32 devices in a mesh: hist: 4 (over y, x), mom: 8 (over z, core).
Axes of the slice: x: 2, y: 2, z: 4, core: 2. Of those that a mesh axis runs over, the one named last changes fastest.
Arguments:
- statistic_now: float32 [256, 1024], P('mom', 'hist'), may hold values from -1.25 to 6.25
- statistic_prev: float32 [256, 1024], P('mom', 'hist'), may hold values from -2 to 7
- spectral_now: float32 [256, 1024], P('mom', 'hist'), may hold values from -1.5 to 1.5
- spectral_prev: float32 [256, 1024], P('mom', 'hist'), may hold values from -1.65 to 1.65
- statistic_hist: bfloat16 [1024, 256, 1024], P('hist', 'mom'), may hold values from -1.5 to 1.5
- spectral_hist: bfloat16 [1024, 256, 1024], P('hist', 'mom'), may hold values from -1.5 to 1.5
Outputs:
- statistic_end: float32 [256, 1024], P('mom', 'hist')
- spectral_end: float32 [256, 1024], P('mom', 'hist')
- memory_stat: float32 [256, 1024], P('mom', 'hist')
- memory_spec: float32 [256, 1024], P('mom', 'hist')
The draws below stay inside these ranges and needn't reach their ends.
All inputs are finite; a program needn't handle non-finite values.
Results may differ from the reference program's by a relative error of at most 0.0029.
Values may be sent and summed in bfloat16 or wider, within the bound.
A program may use at most 128 MiB of HBM per device.

```python
import jax
import jax.numpy as jnp
from jax import lax

P_SIZE = 256
H = 1024
STEPS = 2


def rows_draw(key):
    key_list = jax.random.split(jax.random.fold_in(key, 71), 4)
    ordinal = jnp.arange(P_SIZE, dtype=jnp.float32) + 1.0
    amplitude = 0.5 / jnp.sqrt(0.04 + 4.0 * jnp.sin(jnp.pi * ordinal / (2.0 * (P_SIZE + 1.0))) ** 2)
    stat_now = amplitude[:, None] * (1.0 + 0.5 * jnp.clip(jax.random.normal(key_list[0], (P_SIZE, H), jnp.float32), -3.0, 3.0))
    stat_prev = stat_now + 0.1 * amplitude[:, None] * jnp.clip(jax.random.normal(key_list[1], (P_SIZE, H), jnp.float32), -3.0, 3.0)
    spec_now = 0.5 * jnp.clip(jax.random.normal(key_list[2], (P_SIZE, H), jnp.float32), -3.0, 3.0)
    spec_prev = spec_now + 0.05 * jnp.clip(jax.random.normal(key_list[3], (P_SIZE, H), jnp.float32), -3.0, 3.0)
    return (stat_now, stat_prev, spec_now, spec_prev)


def draw_statistic_now(key, part):
    return rows_draw(key)[0]


def draw_statistic_prev(key, part):
    return rows_draw(key)[1]


def draw_spectral_now(key, part):
    return rows_draw(key)[2]


def draw_spectral_prev(key, part):
    return rows_draw(key)[3]


def draw_spectral_hist(key, part):
    noise_key = jax.random.fold_in(key, 29)
    noise = 0.25 * jnp.clip(jax.random.normal(noise_key, (H, P_SIZE, H), jnp.float32), -4.0, 4.0)
    column = jnp.arange(H, dtype=jnp.float32)
    lift = 0.03 * jnp.clip(column - (H - 17.0), 0.0, 16.0) / 16.0
    return (noise + lift[None, None, :]).astype(jnp.bfloat16)


def steps_of(rng, extent, pieces, least, largest):
    level, own = 1.0, jax.random.fold_in(rng, 6)
    for dim, parts in pieces:
        steps = jnp.exp(jax.random.uniform(jax.random.fold_in(own, dim), (parts,), jnp.float32, least / len(pieces), largest / len(pieces)))
        level = level * jnp.repeat(steps, extent[dim] // parts).reshape([-1 if axis == dim else 1 for axis in range(len(extent))])
    return level


def scatter_about(key, dims, deviation, limit, pieces=(), kind=jnp.bfloat16):
    drawn = jax.random.normal(key, dims, jnp.float32) * deviation
    if len(pieces) > 0:
        drawn = steps_of(key, dims, pieces, -0.22, 0.18) * drawn
    return jnp.clip(drawn, min=-limit, max=limit).astype(kind)


def setup_inputs(seed: int = 0) -> dict:
    key_of = jax.random.split(jax.random.key(seed), 7)
    return {
        "statistic_now": draw_statistic_now(jax.random.fold_in(key_of[6], 71), 0),
        "statistic_prev": draw_statistic_prev(jax.random.fold_in(key_of[6], 71), 0),
        "spectral_now": draw_spectral_now(jax.random.fold_in(key_of[6], 71), 0),
        "spectral_prev": draw_spectral_prev(jax.random.fold_in(key_of[6], 71), 0),
        "statistic_hist": scatter_about(key_of[4], (H, P_SIZE, H), 0.25, 1.5, ((0, 4), (1, 8))),
        "spectral_hist": draw_spectral_hist(jax.random.fold_in(key_of[6], 71), 0),
    }


time_step = 0.2
bare_mass = 0.04
cubic_coupling = 1.0 / 6.0
tadpole_coupling = 2.0

def sine_table(mode_total):
    ordinal = jnp.arange(mode_total, dtype=jnp.float32) + 1.0
    return jnp.sqrt(2.0 / (mode_total + 1.0)) * jnp.sin(jnp.pi * ordinal[:, None] * ordinal[None, :] / (mode_total + 1.0))

def omega_squared(mode_total, offset, amount):
    ordinal = (offset + jnp.arange(amount)).astype(jnp.float32) + 1.0
    return bare_mass + 4.0 * jnp.sin(jnp.pi * ordinal / (2.0 * (mode_total + 1.0))) ** 2

def self_energy(pos_stat, pos_spec):
    square_stat = pos_stat * pos_stat
    square_spec = pos_spec * pos_spec
    return (-cubic_coupling * pos_stat * (square_stat - 0.75 * square_spec), -cubic_coupling * pos_spec * (3.0 * square_stat - 0.25 * square_spec))

def reference(statistic_now, statistic_prev, spectral_now, spectral_prev, statistic_hist, spectral_hist):
    sine_rows = sine_table(P_SIZE)
    frequency = omega_squared(P_SIZE, 0, P_SIZE)[:, None]
    history_times = jnp.arange(H)
    lower_mask = history_times[:, None] <= history_times[None, :]
    upper_mask = history_times[:, None] >= history_times[None, :]
    block_size = 8
    block_count = P_SIZE // block_size

    def integrals(self_stat, self_spec):

        def one_block(block_index):
            first_mode = (block_index * block_size).astype(jnp.int32)
            hist_stat = lax.dynamic_slice_in_dim(statistic_hist, first_mode, block_size, 1).astype(jnp.float32)
            hist_spec = lax.dynamic_slice_in_dim(spectral_hist, first_mode, block_size, 1).astype(jnp.float32)
            weight_stat = lax.dynamic_slice_in_dim(self_stat, first_mode, block_size, 0).astype(jnp.float32)
            weight_spec = lax.dynamic_slice_in_dim(self_spec, first_mode, block_size, 0).astype(jnp.float32)
            spec_low = jnp.where(lower_mask[:, None, :], hist_spec, jnp.zeros((), jnp.float32))
            spec_up = jnp.where(upper_mask[:, None, :], hist_spec, jnp.zeros((), jnp.float32))
            stat_term = jnp.einsum('ps,spu->pu', weight_spec, hist_stat) - jnp.einsum('ps,spu->pu', weight_stat, spec_low)
            spec_term = jnp.einsum('ps,spu->pu', weight_spec, spec_up)
            return (stat_term, spec_term)
        stat_term, spec_term = lax.map(one_block, jnp.arange(block_count, dtype=jnp.int32))
        return (stat_term.reshape(P_SIZE, H), spec_term.reshape(P_SIZE, H))
    stat_row, stat_old = (statistic_now, statistic_prev)
    spec_row, spec_old = (spectral_now, spectral_prev)
    memory_stat = jnp.zeros((P_SIZE, H), jnp.float32)
    memory_spec = jnp.zeros((P_SIZE, H), jnp.float32)
    for step_index in range(STEPS):
        tadpole = tadpole_coupling * jnp.sum(stat_row[:, H - 1]) / P_SIZE
        pos_stat = jnp.dot(sine_rows, stat_row, precision=lax.Precision.HIGHEST, preferred_element_type=jnp.float32)
        pos_spec = jnp.dot(sine_rows, spec_row, precision=lax.Precision.HIGHEST, preferred_element_type=jnp.float32)
        self_stat_pos, self_spec_pos = self_energy(pos_stat, pos_spec)
        self_stat = jnp.dot(sine_rows, self_stat_pos, precision=lax.Precision.HIGHEST, preferred_element_type=jnp.float32).astype(jnp.bfloat16)
        self_spec = jnp.dot(sine_rows, self_spec_pos, precision=lax.Precision.HIGHEST, preferred_element_type=jnp.float32).astype(jnp.bfloat16)
        stat_term, spec_term = integrals(self_stat, self_spec)
        memory_stat = time_step * stat_term
        memory_spec = time_step * spec_term
        new_stat = 2.0 * stat_row - stat_old - time_step * time_step * ((frequency + tadpole) * stat_row + memory_stat)
        new_spec = 2.0 * spec_row - spec_old - time_step * time_step * ((frequency + tadpole) * spec_row + memory_spec)
        stat_old, stat_row = (stat_row, new_stat)
        spec_old, spec_row = (spec_row, new_spec)
    return (stat_row, spec_row, memory_stat, memory_spec)
```

```python
import functools

import jax
import jax.numpy as jnp
import numpy as np
from jax import lax
from jax.experimental import pallas as pl
from jax.experimental.pallas import tpu as pltpu
from jax.sharding import PartitionSpec as P

STEPS = 2


time_step = 0.2
bare_mass = 0.04
cubic_coupling = 1.0 / 6.0
tadpole_coupling = 2.0
highest = lax.Precision.HIGHEST


def broadcast(block, axis, source):
    block = jnp.where(lax.axis_index(axis) == source, block, jnp.zeros_like(block))
    return lax.psum(block, axis)


def sine_table(mode_total):
    ordinal = jnp.arange(mode_total, dtype=jnp.float32) + 1.0
    return jnp.sqrt(2.0 / (mode_total + 1.0)) * jnp.sin(
        jnp.pi * ordinal[:, None] * ordinal[None, :] / (mode_total + 1.0)
    )


def omega_squared(mode_total, offset, amount):
    ordinal = (offset + jnp.arange(amount)).astype(jnp.float32) + 1.0
    return bare_mass + 4.0 * jnp.sin(jnp.pi * ordinal / (2.0 * (mode_total + 1.0))) ** 2


def self_energy(pos_stat, pos_spec):
    square_stat = pos_stat * pos_stat
    square_spec = pos_spec * pos_spec
    return (
        -cubic_coupling * pos_stat * (square_stat - 0.75 * square_spec),
        -cubic_coupling * pos_spec * (3.0 * square_stat - 0.25 * square_spec),
    )


def contract(weights, history):
    return jnp.einsum("ps,spu->pu", weights, history, preferred_element_type=jnp.float32)


def plain_device(
    statistic_now, statistic_prev, spectral_now, spectral_prev, statistic_hist, spectral_hist
):
    mode_count, time_count = statistic_now.shape
    hist_size = lax.axis_size("hist")
    mom_size = lax.axis_size("mom")
    hist_pos = lax.axis_index("hist")
    mom_pos = lax.axis_index("mom")
    mode_total = mode_count * mom_size
    window = statistic_hist.shape[2]
    sine_rows = sine_table(mode_total)
    frequency = omega_squared(mode_total, mom_pos * mode_count, mode_count)[:, None]
    zero_hist = jnp.zeros((), spectral_hist.dtype)
    times_own = hist_pos * time_count + jnp.arange(time_count)
    times_all = jnp.arange(window)
    lower_mask = times_own[:, None] <= times_all[None, :]
    upper_mask = times_own[:, None] >= times_all[None, :]
    spectral_low = jnp.where(lower_mask[:, None, :], spectral_hist, zero_hist)
    spectral_up = jnp.where(upper_mask[:, None, :], spectral_hist, zero_hist)
    stat_row, stat_old = (statistic_now, statistic_prev)
    spec_row, spec_old = (spectral_now, spectral_prev)
    memory_stat = jnp.zeros_like(statistic_now)
    memory_spec = jnp.zeros_like(spectral_now)
    for step_index in range(STEPS):
        partial_value = lax.psum(jnp.sum(stat_row[:, -1]), "mom")
        edge_total = broadcast(partial_value, "hist", hist_size - 1)
        tadpole = tadpole_coupling * edge_total / mode_total
        padded_stat = stat_row
        padded_spec = spec_row
        gather_stat, gather_spec = (
            lax.all_to_all(padded_stat, "mom", split_axis=1, concat_axis=0, tiled=True),
            lax.all_to_all(padded_spec, "mom", split_axis=1, concat_axis=0, tiled=True),
        )
        pos_stat = jnp.dot(
            sine_rows, gather_stat, precision=highest, preferred_element_type=jnp.float32
        )
        pos_spec = jnp.dot(
            sine_rows, gather_spec, precision=highest, preferred_element_type=jnp.float32
        )
        self_stat_pos, self_spec_pos = self_energy(pos_stat, pos_spec)
        back_stat = jnp.dot(
            sine_rows, self_stat_pos, precision=highest, preferred_element_type=jnp.float32
        ).astype(jnp.bfloat16)
        back_spec = jnp.dot(
            sine_rows, self_spec_pos, precision=highest, preferred_element_type=jnp.float32
        ).astype(jnp.bfloat16)
        modes_stat, modes_spec = (
            lax.all_to_all(back_stat, "mom", split_axis=0, concat_axis=1, tiled=True),
            lax.all_to_all(back_spec, "mom", split_axis=0, concat_axis=1, tiled=True),
        )
        part_stat = contract(modes_spec, statistic_hist) - contract(modes_stat, spectral_low)
        part_spec = contract(modes_spec, spectral_up)
        sum_stat, sum_spec = (
            lax.psum_scatter(part_stat, "hist", scatter_dimension=1, tiled=True),
            lax.psum_scatter(part_spec, "hist", scatter_dimension=1, tiled=True),
        )
        memory_stat = time_step * sum_stat
        memory_spec = time_step * sum_spec
        new_stat = (
            2.0 * stat_row
            - stat_old
            - time_step * time_step * ((frequency + tadpole) * stat_row + memory_stat)
        )
        new_spec = (
            2.0 * spec_row
            - spec_old
            - time_step * time_step * ((frequency + tadpole) * spec_row + memory_spec)
        )
        stat_old, stat_row = (stat_row, new_stat)
        spec_old, spec_row = (spec_row, new_spec)
    return (stat_row, spec_row, memory_stat, memory_spec)


LANES = 128
ROWS = 16
MESH = pl.DeviceIdType.MESH


def copy_to(axis, target, source, landing, send_sem, recv_sem):
    return pltpu.make_async_remote_copy(
        src_ref=source,
        dst_ref=landing,
        send_sem=send_sem,
        recv_sem=recv_sem,
        device_id={axis: target},
        device_id_type=MESH,
    )


def fused_kernel(
    hist_size,
    mom_size,
    stat_now_ref,
    stat_prev_ref,
    spec_now_ref,
    spec_prev_ref,
    stat_hist_ref,
    spec_hist_ref,
    forward_ref,
    back_ref,
    frequency_ref,
    stat_end_ref,
    spec_end_ref,
    memory_stat_ref,
    memory_spec_ref,
    stat_held,
    spec_held,
    low_mask,
    up_mask,
    spread,
    weights,
    row_send,
    row_recv,
    self_send,
    self_recv,
    part_send,
    part_recv,
    edge_send,
    edge_recv,
    hist_sem,
    row_sem,
    self_sem,
    part_sem,
    edge_sem,
):
    mode_count, time_count = stat_now_ref.shape
    half = mode_count // 2
    piece = time_count // mom_size
    depth = piece * mode_count
    mode_total = mode_count * mom_size
    here = lax.axis_index("hist")
    me = lax.axis_index("mom")
    order = [*range(1, hist_size), 0]

    loads = {}
    for turn in order:
        column = pl.multiple_of(lax.rem(here + turn, hist_size) * time_count, time_count)
        for which, (whole, held) in enumerate(
            ((stat_hist_ref, stat_held), (spec_hist_ref, spec_held))
        ):
            loads[turn, which] = pltpu.make_async_copy(
                whole.at[:, pl.ds(column, time_count)], held.at[turn], hist_sem.at[which, turn]
            )
            loads[turn, which].start()

    barrier = pltpu.get_barrier_semaphore()
    for offset in range(1, mom_size):
        pl.semaphore_signal(
            barrier, 1, device_id={"mom": lax.rem(me + offset, mom_size)}, device_id_type=MESH
        )
    for offset in range(1, hist_size):
        pl.semaphore_signal(
            barrier, 1, device_id={"hist": lax.rem(here + offset, hist_size)}, device_id_type=MESH
        )
    pl.semaphore_wait(barrier, mom_size + hist_size - 2)

    stat_row, stat_old = stat_now_ref[...], stat_prev_ref[...]
    spec_row, spec_old = spec_now_ref[...], spec_prev_ref[...]
    frequency = frequency_ref[pl.ds(pl.multiple_of(me * mode_count, mode_count), mode_count), :][
        :, 0:1
    ]
    lane = lax.broadcasted_iota(jnp.int32, (1, LANES), 1)
    first_half = lane < 2 * piece
    is_stat = (lane & (2 * piece - 1)) < piece
    sends = []

    for step in range(STEPS):
        edge = jnp.broadcast_to(
            jnp.sum(stat_row[:, time_count - 1 : time_count], axis=0, keepdims=True), (8, LANES)
        )
        for target in range(mom_size):
            span = slice(target * piece, (target + 1) * piece)
            row_send[step, target, 0:half, :] = jnp.concatenate(
                [
                    stat_row[:half, span],
                    spec_row[:half, span],
                    stat_row[half:, span],
                    spec_row[half:, span],
                ],
                axis=1,
            )
            row_send[step, target, half : half + 8, :] = edge
        row_copies = []
        for offset in range(1, mom_size):
            target = lax.rem(me + offset, mom_size)
            source = lax.rem(me + mom_size - offset, mom_size)
            out = copy_to(
                "mom",
                target,
                row_send.at[step, target],
                row_recv.at[step, me],
                row_sem.at[0, step, offset],
                row_sem.at[1, step, me],
            )
            out.start()
            sends.append(out)
            row_copies.append(
                copy_to(
                    "mom",
                    target,
                    row_send.at[step, source],
                    row_recv.at[step, source],
                    row_sem.at[0, step, offset],
                    row_sem.at[1, step, source],
                )
            )
        row_recv[step, me] = row_send[step, me]

        if step == 0:
            place = lax.broadcasted_iota(jnp.int32, (LANES, depth), 0)
            first = lax.broadcasted_iota(jnp.int32, (LANES, depth), 1)
            for kind in range(2):
                for part in range(2):
                    start = part * 2 * piece + (1 - kind) * piece
                    slot = (place - start) * mode_count
                    inside = (first >= slot) & (first < slot + mode_count)
                    spread[2 * kind + part] = jnp.where(
                        inside, 1.0 if kind == 0 else -1.0, 0.0
                    ).astype(jnp.bfloat16)

            late = lax.broadcasted_iota(jnp.int32, (depth, time_count), 1) * mode_count
            entry = lax.broadcasted_iota(jnp.int32, (depth, time_count), 0)

            def fill(block, carry):
                row = entry + block * depth
                span = pl.ds(pl.multiple_of(block * depth, depth), depth)
                low_mask[span, :] = jnp.where(row < late + mode_count, 1.0, 0.0).astype(
                    jnp.bfloat16
                )
                up_mask[span, :] = jnp.where(row >= late, 1.0, 0.0).astype(jnp.bfloat16)
                return carry

            lax.fori_loop(0, mom_size, fill, 0)

        for copy in row_copies:
            copy.wait_recv()
        edge_total = row_recv[step, 0, half : half + 8, :]
        for source in range(1, mom_size):
            edge_total = edge_total + row_recv[step, source, half : half + 8, :]
        edge_send[step] = edge_total
        edge_recv[step, here] = edge_total
        edge_copies = []
        for offset in range(1, hist_size):
            target = lax.rem(here + offset, hist_size)
            source = lax.rem(here + hist_size - offset, hist_size)
            out = copy_to(
                "hist",
                target,
                edge_send.at[step],
                edge_recv.at[step, here],
                edge_sem.at[0, step, offset],
                edge_sem.at[1, step, here],
            )
            out.start()
            sends.append(out)
            edge_copies.append(
                copy_to(
                    "hist",
                    target,
                    edge_send.at[step],
                    edge_recv.at[step, source],
                    edge_sem.at[0, step, offset],
                    edge_sem.at[1, step, source],
                )
            )

        rows = row_recv[step, :, 0:half, :].reshape(mom_size * half, LANES)
        both = jnp.dot(
            forward_ref[...], rows, precision=highest, preferred_element_type=jnp.float32
        )
        chosen = jnp.where(first_half, both[:mode_total], both[mode_total:])
        pos = chosen + pltpu.roll(chosen, 2 * piece, 1)
        swapped = pltpu.roll(pos, piece, 1)
        pos_stat = jnp.where(is_stat, pos, swapped)
        pos_spec = jnp.where(is_stat, swapped, pos)
        self_stat, self_spec = self_energy(pos_stat, pos_spec)
        both = jnp.dot(
            back_ref[...],
            jnp.where(is_stat, self_stat, self_spec),
            precision=highest,
            preferred_element_type=jnp.float32,
        )
        self_rows = jnp.where(first_half, both[: mom_size * half], both[mom_size * half :])
        self_send[step] = self_rows.astype(jnp.bfloat16).reshape(mom_size, half, LANES)
        self_copies = []
        for offset in range(1, mom_size):
            target = lax.rem(me + offset, mom_size)
            source = lax.rem(me + mom_size - offset, mom_size)
            out = copy_to(
                "mom",
                target,
                self_send.at[step, target],
                self_recv.at[step, me],
                self_sem.at[0, step, offset],
                self_sem.at[1, step, me],
            )
            out.start()
            sends.append(out)
            self_copies.append(
                copy_to(
                    "mom",
                    target,
                    self_send.at[step, source],
                    self_recv.at[step, source],
                    self_sem.at[0, step, offset],
                    self_sem.at[1, step, source],
                )
            )
        self_recv[step, me] = self_send[step, me]
        for copy in self_copies:
            copy.wait_recv()

        arrived = self_recv[step].reshape(mom_size * half, LANES)
        mode = lax.broadcasted_iota(jnp.int32, (mom_size * half, depth), 1) & (mode_count - 1)
        owner = lax.broadcasted_iota(jnp.int32, (mom_size * half, depth), 0) & (half - 1)
        for kind in range(2):
            for part in range(2):
                wide = jnp.dot(
                    arrived, spread[2 * kind + part], preferred_element_type=jnp.float32
                )
                wide = jnp.where(mode == owner + part * half, wide, 0.0).astype(jnp.bfloat16)
                begin = kind * mode_count + part * half
                weights[:, begin : begin + half, :] = wide.reshape(mom_size, half, depth)

        zeros = jnp.zeros((mode_count, time_count), jnp.float32)
        part_copies = []
        for turn in order:
            if step == 0:
                loads[turn, 0].wait()
                loads[turn, 1].wait()
            if turn:
                target = lax.rem(here + turn, hist_size)
                source = lax.rem(here + hist_size - turn, hist_size)
                wrapped = (here + turn) // hist_size
                select = pl.multiple_of((1 - wrapped) * mode_count, mode_count)

                def add(block, sums):
                    span = pl.ds(pl.multiple_of(block * depth, depth), depth)
                    return (
                        sums[0]
                        + jnp.dot(
                            weights[block, 0:mode_count, :],
                            stat_held[turn, span, :],
                            preferred_element_type=jnp.float32,
                        ),
                        sums[1]
                        + jnp.dot(
                            weights[block, pl.ds(select, mode_count), :],
                            spec_held[turn, span, :],
                            preferred_element_type=jnp.float32,
                        ),
                    )

                stat_sum, spec_sum = lax.fori_loop(0, mom_size, add, (zeros, zeros))
                below = wrapped.astype(jnp.float32)
                part_send[step, turn, 0:mode_count, :] = (
                    stat_sum + (1.0 - below) * spec_sum
                ).astype(jnp.bfloat16)
                part_send[step, turn, mode_count:, :] = (below * spec_sum).astype(jnp.bfloat16)
                out = copy_to(
                    "hist",
                    target,
                    part_send.at[step, turn],
                    part_recv.at[step, here],
                    part_sem.at[0, step, turn],
                    part_sem.at[1, step, here],
                )
                out.start()
                sends.append(out)
                part_copies.append(
                    (
                        source,
                        copy_to(
                            "hist",
                            target,
                            part_send.at[step, turn],
                            part_recv.at[step, source],
                            part_sem.at[0, step, turn],
                            part_sem.at[1, step, source],
                        ),
                    )
                )
            else:

                def add_own(block, sums):
                    span = pl.ds(pl.multiple_of(block * depth, depth), depth)
                    rho = spec_held[0, span, :]
                    own = weights[block, 0:mode_count, :]
                    return (
                        sums[0]
                        + jnp.dot(own, stat_held[0, span, :], preferred_element_type=jnp.float32)
                        + jnp.dot(
                            weights[block, mode_count:, :],
                            rho * low_mask[span, :],
                            preferred_element_type=jnp.float32,
                        ),
                        sums[1]
                        + jnp.dot(
                            own, rho * up_mask[span, :], preferred_element_type=jnp.float32
                        ),
                    )

                stat_sum, spec_sum = lax.fori_loop(0, mom_size, add_own, (zeros, zeros))

        for copy in edge_copies:
            copy.wait_recv()
        tadpole = (tadpole_coupling / mode_total) * edge_recv[step, hist_size - 1][0:1, 0:1]
        for source, copy in part_copies:
            copy.wait_recv()
            stat_sum = stat_sum + part_recv[step, source, 0:mode_count, :].astype(jnp.float32)
            spec_sum = spec_sum + part_recv[step, source, mode_count:, :].astype(jnp.float32)
        memory_stat = time_step * stat_sum
        memory_spec = time_step * spec_sum
        square = time_step * time_step
        stiffness = frequency + tadpole
        new_stat = 2.0 * stat_row - stat_old - square * (stiffness * stat_row + memory_stat)
        new_spec = 2.0 * spec_row - spec_old - square * (stiffness * spec_row + memory_spec)
        stat_old, stat_row = stat_row, new_stat
        spec_old, spec_row = spec_row, new_spec

    stat_end_ref[...] = stat_row
    spec_end_ref[...] = spec_row
    memory_stat_ref[...] = memory_stat
    memory_spec_ref[...] = memory_spec
    for out in sends:
        out.wait_send()


def sine_blocks(mode_total, mom_size):
    ordinal = np.arange(mode_total, dtype=np.float64) + 1.0
    sine = np.sqrt(2.0 / (mode_total + 1.0)) * np.sin(
        np.pi * ordinal[:, None] * ordinal[None, :] / (mode_total + 1.0)
    )
    split = sine.reshape(mode_total, mom_size, 2, -1)
    lower = split[:, :, 0, :].reshape(mode_total, -1)
    upper = split[:, :, 1, :].reshape(mode_total, -1)
    forward = np.concatenate([lower, upper], axis=0)
    back = np.concatenate([lower.T, upper.T], axis=0)
    frequency = bare_mass + 4.0 * np.sin(np.pi * ordinal / (2.0 * (mode_total + 1.0))) ** 2
    frequency = np.repeat(frequency[:, None], LANES, axis=1)
    return tuple(np.ascontiguousarray(a, np.float32) for a in (forward, back, frequency))


def per_device(
    statistic_now, statistic_prev, spectral_now, spectral_prev, statistic_hist, spectral_hist
):
    mode_count, time_count = statistic_now.shape
    hist_size = lax.axis_size("hist")
    mom_size = lax.axis_size("mom")
    window = statistic_hist.shape[2]
    piece = time_count // mom_size
    half = mode_count // 2
    fits = (
        4 * piece * mom_size == LANES * mom_size
        and half % ROWS == 0
        and mode_count & (mode_count - 1) == 0
        and time_count % LANES == 0
        and hist_size > 1
        and mom_size > 1
    )
    if not fits:
        return plain_device(
            statistic_now, statistic_prev, spectral_now, spectral_prev, statistic_hist, spectral_hist
        )
    mode_total = mode_count * mom_size
    total = time_count * mode_count
    depth = piece * mode_count
    constants = sine_blocks(mode_total, mom_size)
    vmem = pl.BlockSpec(memory_space=pltpu.VMEM)
    far = pl.BlockSpec(memory_space=pl.ANY)
    dma = pltpu.SemaphoreType.DMA
    return pl.pallas_call(
        functools.partial(fused_kernel, hist_size, mom_size),
        out_shape=(jax.ShapeDtypeStruct((mode_count, time_count), jnp.float32),) * 4,
        in_specs=[vmem] * 4 + [far] * 2 + [vmem] * 3,
        out_specs=(vmem,) * 4,
        scratch_shapes=[
            pltpu.VMEM((hist_size, total, time_count), jnp.bfloat16),
            pltpu.VMEM((hist_size, total, time_count), jnp.bfloat16),
            pltpu.VMEM((total, time_count), jnp.bfloat16),
            pltpu.VMEM((total, time_count), jnp.bfloat16),
            pltpu.VMEM((4, LANES, depth), jnp.bfloat16),
            pltpu.VMEM((mom_size, 2 * mode_count, depth), jnp.bfloat16),
            pltpu.VMEM((STEPS, mom_size, half + 8, LANES), jnp.float32),
            pltpu.VMEM((STEPS, mom_size, half + 8, LANES), jnp.float32),
            pltpu.VMEM((STEPS, mom_size, half, LANES), jnp.bfloat16),
            pltpu.VMEM((STEPS, mom_size, half, LANES), jnp.bfloat16),
            pltpu.VMEM((STEPS, hist_size, 2 * mode_count, time_count), jnp.bfloat16),
            pltpu.VMEM((STEPS, hist_size, 2 * mode_count, time_count), jnp.bfloat16),
            pltpu.VMEM((STEPS, 8, LANES), jnp.float32),
            pltpu.VMEM((STEPS, hist_size, 8, LANES), jnp.float32),
            dma((2, hist_size)),
            dma((2, STEPS, mom_size)),
            dma((2, STEPS, mom_size)),
            dma((2, STEPS, hist_size)),
            dma((2, STEPS, hist_size)),
        ],
        compiler_params=pltpu.CompilerParams(
            collective_id=0, has_side_effects=True, vmem_limit_bytes=56 * 1024 * 1024
        ),
        cost_estimate=pl.CostEstimate(
            flops=STEPS * 6 * total * window, bytes_accessed=4 * total * window, transcendentals=0
        ),
    )(
        statistic_now,
        statistic_prev,
        spectral_now,
        spectral_prev,
        statistic_hist.reshape(total, window),
        spectral_hist.reshape(total, window),
        *constants,
    )


def solution(mesh):
    placed = (
        P("mom", "hist"),
        P("mom", "hist"),
        P("mom", "hist"),
        P("mom", "hist"),
        P("hist", "mom", None),
        P("hist", "mom", None),
    )
    return jax.shard_map(
        per_device,
        mesh=mesh,
        in_specs=placed,
        out_specs=(P("mom", "hist"), P("mom", "hist"), P("mom", "hist"), P("mom", "hist")),
        check_vma=False,
    )
```

```python
import functools

import jax
import jax.numpy as jnp
import numpy as np
from jax import lax
from jax.experimental import pallas as pl
from jax.experimental.pallas import tpu as pltpu
from jax.sharding import PartitionSpec as P

STEPS = 2


time_step = 0.2
bare_mass = 0.04
cubic_coupling = 1.0 / 6.0
tadpole_coupling = 2.0
highest = lax.Precision.HIGHEST


def broadcast(block, axis, source):
    block = jnp.where(lax.axis_index(axis) == source, block, jnp.zeros_like(block))
    return lax.psum(block, axis)


def sine_table(mode_total):
    ordinal = jnp.arange(mode_total, dtype=jnp.float32) + 1.0
    return jnp.sqrt(2.0 / (mode_total + 1.0)) * jnp.sin(
        jnp.pi * ordinal[:, None] * ordinal[None, :] / (mode_total + 1.0)
    )


def omega_squared(mode_total, offset, amount):
    ordinal = (offset + jnp.arange(amount)).astype(jnp.float32) + 1.0
    return bare_mass + 4.0 * jnp.sin(jnp.pi * ordinal / (2.0 * (mode_total + 1.0))) ** 2


def self_energy(pos_stat, pos_spec):
    square_stat = pos_stat * pos_stat
    square_spec = pos_spec * pos_spec
    return (
        -cubic_coupling * pos_stat * (square_stat - 0.75 * square_spec),
        -cubic_coupling * pos_spec * (3.0 * square_stat - 0.25 * square_spec),
    )


def contract(weights, history):
    return jnp.einsum("ps,spu->pu", weights, history, preferred_element_type=jnp.float32)


def plain_device(
    statistic_now, statistic_prev, spectral_now, spectral_prev, statistic_hist, spectral_hist
):
    mode_count, time_count = statistic_now.shape
    hist_size = lax.axis_size("hist")
    mom_size = lax.axis_size("mom")
    hist_pos = lax.axis_index("hist")
    mom_pos = lax.axis_index("mom")
    mode_total = mode_count * mom_size
    window = statistic_hist.shape[2]
    sine_rows = sine_table(mode_total)
    frequency = omega_squared(mode_total, mom_pos * mode_count, mode_count)[:, None]
    zero_hist = jnp.zeros((), spectral_hist.dtype)
    times_own = hist_pos * time_count + jnp.arange(time_count)
    times_all = jnp.arange(window)
    lower_mask = times_own[:, None] <= times_all[None, :]
    upper_mask = times_own[:, None] >= times_all[None, :]
    spectral_low = jnp.where(lower_mask[:, None, :], spectral_hist, zero_hist)
    spectral_up = jnp.where(upper_mask[:, None, :], spectral_hist, zero_hist)
    stat_row, stat_old = (statistic_now, statistic_prev)
    spec_row, spec_old = (spectral_now, spectral_prev)
    memory_stat = jnp.zeros_like(statistic_now)
    memory_spec = jnp.zeros_like(spectral_now)
    for step_index in range(STEPS):
        partial_value = lax.psum(jnp.sum(stat_row[:, -1]), "mom")
        edge_total = broadcast(partial_value, "hist", hist_size - 1)
        tadpole = tadpole_coupling * edge_total / mode_total
        padded_stat = stat_row
        padded_spec = spec_row
        gather_stat, gather_spec = (
            lax.all_to_all(padded_stat, "mom", split_axis=1, concat_axis=0, tiled=True),
            lax.all_to_all(padded_spec, "mom", split_axis=1, concat_axis=0, tiled=True),
        )
        pos_stat = jnp.dot(
            sine_rows, gather_stat, precision=highest, preferred_element_type=jnp.float32
        )
        pos_spec = jnp.dot(
            sine_rows, gather_spec, precision=highest, preferred_element_type=jnp.float32
        )
        self_stat_pos, self_spec_pos = self_energy(pos_stat, pos_spec)
        back_stat = jnp.dot(
            sine_rows, self_stat_pos, precision=highest, preferred_element_type=jnp.float32
        ).astype(jnp.bfloat16)
        back_spec = jnp.dot(
            sine_rows, self_spec_pos, precision=highest, preferred_element_type=jnp.float32
        ).astype(jnp.bfloat16)
        modes_stat, modes_spec = (
            lax.all_to_all(back_stat, "mom", split_axis=0, concat_axis=1, tiled=True),
            lax.all_to_all(back_spec, "mom", split_axis=0, concat_axis=1, tiled=True),
        )
        part_stat = contract(modes_spec, statistic_hist) - contract(modes_stat, spectral_low)
        part_spec = contract(modes_spec, spectral_up)
        sum_stat, sum_spec = (
            lax.psum_scatter(part_stat, "hist", scatter_dimension=1, tiled=True),
            lax.psum_scatter(part_spec, "hist", scatter_dimension=1, tiled=True),
        )
        memory_stat = time_step * sum_stat
        memory_spec = time_step * sum_spec
        new_stat = (
            2.0 * stat_row
            - stat_old
            - time_step * time_step * ((frequency + tadpole) * stat_row + memory_stat)
        )
        new_spec = (
            2.0 * spec_row
            - spec_old
            - time_step * time_step * ((frequency + tadpole) * spec_row + memory_spec)
        )
        stat_old, stat_row = (stat_row, new_stat)
        spec_old, spec_row = (spec_row, new_spec)
    return (stat_row, spec_row, memory_stat, memory_spec)


LANES = 128
ROWS = 16
MESH = pl.DeviceIdType.MESH


def copy_to(axis, target, source, landing, send_sem, recv_sem):
    return pltpu.make_async_remote_copy(
        src_ref=source,
        dst_ref=landing,
        send_sem=send_sem,
        recv_sem=recv_sem,
        device_id={axis: target},
        device_id_type=MESH,
    )


def fused_kernel(
    hist_size,
    mom_size,
    stat_now_ref,
    stat_prev_ref,
    spec_now_ref,
    spec_prev_ref,
    stat_hist_ref,
    spec_hist_ref,
    forward_ref,
    back_ref,
    frequency_ref,
    result_ref,
    stat_held,
    spec_held,
    low_mask,
    up_mask,
    spread,
    weights,
    row_send,
    row_recv,
    self_send,
    self_recv,
    part_send,
    part_recv,
    edge_send,
    edge_recv,
    hist_sem,
    row_sem,
    self_sem,
    part_sem,
    edge_sem,
    mode_send,
    mode_recv,
    mode_sem,
):
    mode_count, time_count = stat_now_ref.shape
    half = mode_count // 2
    piece = time_count // mom_size
    depth = piece * mode_count
    mode_total = mode_count * mom_size
    here = lax.axis_index("hist")
    me = lax.axis_index("mom")
    order = [*range(1, hist_size), 0]
    rounds = 2 if mom_size % 2 == 0 else 1
    round_depth = mom_size * depth // rounds

    loads = {}
    for turn in order:
        column = pl.multiple_of(lax.rem(here + turn, hist_size) * time_count, time_count)
        for which, (whole, held) in enumerate(
            ((stat_hist_ref, stat_held), (spec_hist_ref, spec_held))
        ):
            loads[turn, which] = pltpu.make_async_copy(
                whole.at[:, pl.ds(column, time_count)], held.at[turn], hist_sem.at[which, turn]
            )
            loads[turn, which].start()

    barrier = pltpu.get_barrier_semaphore()
    for offset in range(1, mom_size):
        pl.semaphore_signal(
            barrier, 1, device_id={"mom": lax.rem(me + offset, mom_size)}, device_id_type=MESH
        )
    for offset in range(1, hist_size):
        pl.semaphore_signal(
            barrier, 1, device_id={"hist": lax.rem(here + offset, hist_size)}, device_id_type=MESH
        )

    place = lax.broadcasted_iota(jnp.int32, (LANES, depth), 0)
    first = lax.broadcasted_iota(jnp.int32, (LANES, depth), 1)
    for kind in range(2):
        for part in range(2):
            start = part * 2 * piece + (1 - kind) * piece
            slot = (place - start) * mode_count
            inside = (first >= slot) & (first < slot + mode_count)
            spread[2 * kind + part] = jnp.where(
                inside, 1.0 if kind == 0 else -1.0, 0.0
            ).astype(jnp.bfloat16)

    stat_row, stat_old = stat_now_ref[...], stat_prev_ref[...]
    spec_row, spec_old = spec_now_ref[...], spec_prev_ref[...]
    frequency = frequency_ref[pl.ds(pl.multiple_of(me * mode_count, mode_count), mode_count), :][
        :, 0:1
    ]
    lane = lax.broadcasted_iota(jnp.int32, (1, LANES), 1)
    first_half = lane < 2 * piece
    is_stat = (lane & (2 * piece - 1)) < piece
    sends = []

    for step in range(STEPS):
        edge = jnp.broadcast_to(
            jnp.sum(stat_row[:, time_count - 1 : time_count], axis=0, keepdims=True), (8, LANES)
        )
        for target in range(mom_size):
            span = slice(target * piece, (target + 1) * piece)
            row_send[step, target] = jnp.concatenate(
                [
                    stat_row[:half, span],
                    spec_row[:half, span],
                    stat_row[half:, span],
                    spec_row[half:, span],
                ],
                axis=1,
            )
        if step == 0:
            pl.semaphore_wait(barrier, mom_size + hist_size - 2)
        row_copies = []
        for offset in range(1, mom_size):
            target = lax.rem(me + offset, mom_size)
            source = lax.rem(me + mom_size - offset, mom_size)
            out = copy_to(
                "mom",
                target,
                row_send.at[step, target],
                row_recv.at[step, me],
                row_sem.at[0, step, offset],
                row_sem.at[1, step, me],
            )
            out.start()
            sends.append(out)
            row_copies.append(
                copy_to(
                    "mom",
                    target,
                    row_send.at[step, source],
                    row_recv.at[step, source],
                    row_sem.at[0, step, offset],
                    row_sem.at[1, step, source],
                )
            )
        row_recv[step, me] = row_send[step, me]
        mode_send[step] = edge
        mode_recv[step, me] = edge
        mode_copies = []
        for offset in range(1, mom_size):
            target = lax.rem(me + offset, mom_size)
            source = lax.rem(me + mom_size - offset, mom_size)
            out = copy_to(
                "mom",
                target,
                mode_send.at[step],
                mode_recv.at[step, me],
                mode_sem.at[0, step, offset],
                mode_sem.at[1, step, me],
            )
            out.start()
            sends.append(out)
            mode_copies.append(
                copy_to(
                    "mom",
                    target,
                    mode_send.at[step],
                    mode_recv.at[step, source],
                    mode_sem.at[0, step, offset],
                    mode_sem.at[1, step, source],
                )
            )

        if step == 0:
            late = lax.broadcasted_iota(jnp.int32, (depth, time_count), 1) * mode_count
            entry = lax.broadcasted_iota(jnp.int32, (depth, time_count), 0)

            def fill(block, carry):
                row = entry + block * depth
                span = pl.ds(pl.multiple_of(block * depth, depth), depth)
                low_mask[span, :] = jnp.where(row < late + mode_count, 1.0, 0.0).astype(
                    jnp.bfloat16
                )
                up_mask[span, :] = jnp.where(row >= late, 1.0, 0.0).astype(jnp.bfloat16)
                return carry

            lax.fori_loop(0, mom_size, fill, 0)

        for copy in row_copies:
            copy.wait_recv()
        rows = row_recv[step].reshape(mom_size * half, LANES)
        both = jnp.dot(
            forward_ref[...], rows, precision=highest, preferred_element_type=jnp.float32
        )
        chosen = jnp.where(first_half, both[:mode_total], both[mode_total:])
        pos = chosen + pltpu.roll(chosen, 2 * piece, 1)
        swapped = pltpu.roll(pos, piece, 1)
        pos_stat = jnp.where(is_stat, pos, swapped)
        pos_spec = jnp.where(is_stat, swapped, pos)
        self_stat, self_spec = self_energy(pos_stat, pos_spec)
        both = jnp.dot(
            back_ref[...],
            jnp.where(is_stat, self_stat, self_spec),
            precision=highest,
            preferred_element_type=jnp.float32,
        )
        self_rows = jnp.where(first_half, both[: mom_size * half], both[mom_size * half :])
        self_send[step] = self_rows.astype(jnp.bfloat16).reshape(mom_size, half, LANES)
        self_copies = []
        for offset in range(1, mom_size):
            target = lax.rem(me + offset, mom_size)
            source = lax.rem(me + mom_size - offset, mom_size)
            out = copy_to(
                "mom",
                target,
                self_send.at[step, target],
                self_recv.at[step, me],
                self_sem.at[0, step, offset],
                self_sem.at[1, step, me],
            )
            out.start()
            sends.append(out)
            self_copies.append(
                copy_to(
                    "mom",
                    target,
                    self_send.at[step, source],
                    self_recv.at[step, source],
                    self_sem.at[0, step, offset],
                    self_sem.at[1, step, source],
                )
            )
        self_recv[step, me] = self_send[step, me]
        for copy in mode_copies:
            copy.wait_recv()
        edge_total = jnp.sum(mode_recv[step], axis=0)
        edge_send[step] = edge_total
        edge_recv[step, here] = edge_total
        edge_copies = []
        for offset in range(1, hist_size):
            target = lax.rem(here + offset, hist_size)
            source = lax.rem(here + hist_size - offset, hist_size)
            out = copy_to(
                "hist",
                target,
                edge_send.at[step],
                edge_recv.at[step, here],
                edge_sem.at[0, step, offset],
                edge_sem.at[1, step, here],
            )
            out.start()
            sends.append(out)
            edge_copies.append(
                copy_to(
                    "hist",
                    target,
                    edge_send.at[step],
                    edge_recv.at[step, source],
                    edge_sem.at[0, step, offset],
                    edge_sem.at[1, step, source],
                )
            )

        for copy in self_copies:
            copy.wait_recv()

        arrived = self_recv[step].reshape(mom_size * half, LANES)
        mode = lax.broadcasted_iota(jnp.int32, (mom_size * half, depth), 1) & (mode_count - 1)
        owner = lax.broadcasted_iota(jnp.int32, (mom_size * half, depth), 0) & (half - 1)
        for kind in range(2):
            for part in range(2):
                wide = jnp.dot(
                    arrived, spread[2 * kind + part], preferred_element_type=jnp.float32
                )
                wide = jnp.where(mode == owner + part * half, wide, 0.0).astype(jnp.bfloat16)
                begin = kind * mode_count + part * half
                for block in range(mom_size):
                    weights[begin : begin + half, block * depth : (block + 1) * depth] = wide[
                        block * half : (block + 1) * half
                    ]

        zeros = jnp.zeros((mode_count, time_count), jnp.float32)
        part_copies = []
        for turn in order:
            if step == 0:
                loads[turn, 0].wait()
                loads[turn, 1].wait()
            if turn:
                target = lax.rem(here + turn, hist_size)
                source = lax.rem(here + hist_size - turn, hist_size)
                wrapped = (here + turn) // hist_size
                select = pl.multiple_of((1 - wrapped) * mode_count, mode_count)

                def add(block, sums):
                    span = pl.ds(pl.multiple_of(block * round_depth, round_depth), round_depth)
                    return (
                        sums[0]
                        + jnp.dot(
                            weights[0:mode_count, span],
                            stat_held[turn, span, :],
                            preferred_element_type=jnp.float32,
                        ),
                        sums[1]
                        + jnp.dot(
                            weights[pl.ds(select, mode_count), span],
                            spec_held[turn, span, :],
                            preferred_element_type=jnp.float32,
                        ),
                    )

                stat_sum, spec_sum = lax.fori_loop(0, rounds, add, (zeros, zeros))
                below = wrapped.astype(jnp.float32)
                part_send[step, turn, 0:mode_count, :] = (
                    stat_sum + (1.0 - below) * spec_sum
                ).astype(jnp.bfloat16)
                part_send[step, turn, mode_count:, :] = (below * spec_sum).astype(jnp.bfloat16)
                out = copy_to(
                    "hist",
                    target,
                    part_send.at[step, turn],
                    part_recv.at[step, here],
                    part_sem.at[0, step, turn],
                    part_sem.at[1, step, here],
                )
                out.start()
                sends.append(out)
                part_copies.append(
                    (
                        source,
                        copy_to(
                            "hist",
                            target,
                            part_send.at[step, turn],
                            part_recv.at[step, source],
                            part_sem.at[0, step, turn],
                            part_sem.at[1, step, source],
                        ),
                    )
                )
            else:

                def add_own(block, sums):
                    span = pl.ds(pl.multiple_of(block * round_depth, round_depth), round_depth)
                    rho = spec_held[0, span, :]
                    own = weights[0:mode_count, span]
                    return (
                        sums[0]
                        + jnp.dot(own, stat_held[0, span, :], preferred_element_type=jnp.float32)
                        + jnp.dot(
                            weights[mode_count:, span],
                            rho * low_mask[span, :],
                            preferred_element_type=jnp.float32,
                        ),
                        sums[1]
                        + jnp.dot(
                            own, rho * up_mask[span, :], preferred_element_type=jnp.float32
                        ),
                    )

                stat_sum, spec_sum = lax.fori_loop(0, rounds, add_own, (zeros, zeros))

        for copy in edge_copies:
            copy.wait_recv()
        tadpole = (tadpole_coupling / mode_total) * edge_recv[step, hist_size - 1][0:1, 0:1]
        for source, copy in part_copies:
            copy.wait_recv()
            stat_sum = stat_sum + part_recv[step, source, 0:mode_count, :].astype(jnp.float32)
            spec_sum = spec_sum + part_recv[step, source, mode_count:, :].astype(jnp.float32)
        memory_stat = time_step * stat_sum
        memory_spec = time_step * spec_sum
        square = time_step * time_step
        stiffness = frequency + tadpole
        new_stat = 2.0 * stat_row - stat_old - square * (stiffness * stat_row + memory_stat)
        new_spec = 2.0 * spec_row - spec_old - square * (stiffness * spec_row + memory_spec)
        stat_old, stat_row = stat_row, new_stat
        spec_old, spec_row = spec_row, new_spec

    for place, value in enumerate((stat_row, spec_row, memory_stat, memory_spec)):
        result_ref[place] = value
    for out in sends:
        out.wait_send()


def split_kernel(packed_ref, *refs):
    *results, sem = refs
    copies = [
        pltpu.make_async_copy(packed_ref.at[place], result, sem.at[place])
        for place, result in enumerate(results)
    ]
    for copy in copies:
        copy.start()
    for copy in copies:
        copy.wait()


def sine_blocks(mode_total, mom_size):
    ordinal = np.arange(mode_total, dtype=np.float64) + 1.0
    sine = np.sqrt(2.0 / (mode_total + 1.0)) * np.sin(
        np.pi * ordinal[:, None] * ordinal[None, :] / (mode_total + 1.0)
    )
    split = sine.reshape(mode_total, mom_size, 2, -1)
    lower = split[:, :, 0, :].reshape(mode_total, -1)
    upper = split[:, :, 1, :].reshape(mode_total, -1)
    forward = np.concatenate([lower, upper], axis=0)
    back = np.concatenate([lower.T, upper.T], axis=0)
    frequency = bare_mass + 4.0 * np.sin(np.pi * ordinal / (2.0 * (mode_total + 1.0))) ** 2
    frequency = np.repeat(frequency[:, None], LANES, axis=1)
    return tuple(np.ascontiguousarray(a, np.float32) for a in (forward, back, frequency))


def per_device(
    statistic_now, statistic_prev, spectral_now, spectral_prev, statistic_hist, spectral_hist
):
    mode_count, time_count = statistic_now.shape
    hist_size = lax.axis_size("hist")
    mom_size = lax.axis_size("mom")
    window = statistic_hist.shape[2]
    piece = time_count // mom_size
    half = mode_count // 2
    fits = (
        4 * piece * mom_size == LANES * mom_size
        and half % ROWS == 0
        and mode_count & (mode_count - 1) == 0
        and time_count % LANES == 0
        and hist_size > 1
        and mom_size > 1
    )
    if not fits:
        return plain_device(
            statistic_now, statistic_prev, spectral_now, spectral_prev, statistic_hist, spectral_hist
        )
    mode_total = mode_count * mom_size
    total = time_count * mode_count
    depth = piece * mode_count
    constants = sine_blocks(mode_total, mom_size)
    vmem = pl.BlockSpec(memory_space=pltpu.VMEM)
    far = pl.BlockSpec(memory_space=pl.ANY)
    dma = pltpu.SemaphoreType.DMA
    packed = pl.pallas_call(
        functools.partial(fused_kernel, hist_size, mom_size),
        out_shape=jax.ShapeDtypeStruct((4, mode_count, time_count), jnp.float32),
        in_specs=[vmem] * 4 + [far] * 2 + [vmem] * 3,
        out_specs=vmem,
        scratch_shapes=[
            pltpu.VMEM((hist_size, total, time_count), jnp.bfloat16),
            pltpu.VMEM((hist_size, total, time_count), jnp.bfloat16),
            pltpu.VMEM((total, time_count), jnp.bfloat16),
            pltpu.VMEM((total, time_count), jnp.bfloat16),
            pltpu.VMEM((4, LANES, depth), jnp.bfloat16),
            pltpu.VMEM((2 * mode_count, total), jnp.bfloat16),
            pltpu.VMEM((STEPS, mom_size, half, LANES), jnp.float32),
            pltpu.VMEM((STEPS, mom_size, half, LANES), jnp.float32),
            pltpu.VMEM((STEPS, mom_size, half, LANES), jnp.bfloat16),
            pltpu.VMEM((STEPS, mom_size, half, LANES), jnp.bfloat16),
            pltpu.VMEM((STEPS, hist_size, 2 * mode_count, time_count), jnp.bfloat16),
            pltpu.VMEM((STEPS, hist_size, 2 * mode_count, time_count), jnp.bfloat16),
            pltpu.VMEM((STEPS, 8, LANES), jnp.float32),
            pltpu.VMEM((STEPS, hist_size, 8, LANES), jnp.float32),
            dma((2, hist_size)),
            dma((2, STEPS, mom_size)),
            dma((2, STEPS, mom_size)),
            dma((2, STEPS, hist_size)),
            dma((2, STEPS, hist_size)),
            pltpu.VMEM((STEPS, 8, LANES), jnp.float32),
            pltpu.VMEM((STEPS, mom_size, 8, LANES), jnp.float32),
            dma((2, STEPS, mom_size)),
        ],
        compiler_params=pltpu.CompilerParams(
            collective_id=0, has_side_effects=True, vmem_limit_bytes=56 * 1024 * 1024
        ),
        cost_estimate=pl.CostEstimate(
            flops=STEPS * 6 * total * window, bytes_accessed=4 * total * window, transcendentals=0
        ),
    )(
        statistic_now,
        statistic_prev,
        spectral_now,
        spectral_prev,
        statistic_hist.reshape(total, window),
        spectral_hist.reshape(total, window),
        *constants,
    )
    return pl.pallas_call(
        split_kernel,
        out_shape=(jax.ShapeDtypeStruct((mode_count, time_count), jnp.float32),) * 4,
        in_specs=[far],
        out_specs=(far,) * 4,
        scratch_shapes=[dma((4,))],
    )(packed)


def solution(mesh):
    placed = (
        P("mom", "hist"),
        P("mom", "hist"),
        P("mom", "hist"),
        P("mom", "hist"),
        P("hist", "mom", None),
        P("hist", "mom", None),
    )
    return jax.shard_map(
        per_device,
        mesh=mesh,
        in_specs=placed,
        out_specs=(P("mom", "hist"), P("mom", "hist"), P("mom", "hist"), P("mom", "hist")),
        check_vma=False,
    )
```

```python
import functools

import jax
import jax.numpy as jnp
import numpy as np
from jax import lax
from jax.experimental import pallas as pl
from jax.experimental.pallas import tpu as pltpu
from jax.sharding import PartitionSpec as P

STEPS = 2


time_step = 0.2
bare_mass = 0.04
cubic_coupling = 1.0 / 6.0
tadpole_coupling = 2.0
highest = lax.Precision.HIGHEST


def broadcast(block, axis, source):
    block = jnp.where(lax.axis_index(axis) == source, block, jnp.zeros_like(block))
    return lax.psum(block, axis)


def sine_table(mode_total):
    ordinal = jnp.arange(mode_total, dtype=jnp.float32) + 1.0
    return jnp.sqrt(2.0 / (mode_total + 1.0)) * jnp.sin(
        jnp.pi * ordinal[:, None] * ordinal[None, :] / (mode_total + 1.0)
    )


def omega_squared(mode_total, offset, amount):
    ordinal = (offset + jnp.arange(amount)).astype(jnp.float32) + 1.0
    return bare_mass + 4.0 * jnp.sin(jnp.pi * ordinal / (2.0 * (mode_total + 1.0))) ** 2


def self_energy(pos_stat, pos_spec):
    square_stat = pos_stat * pos_stat
    square_spec = pos_spec * pos_spec
    return (
        -cubic_coupling * pos_stat * (square_stat - 0.75 * square_spec),
        -cubic_coupling * pos_spec * (3.0 * square_stat - 0.25 * square_spec),
    )


def contract(weights, history):
    return jnp.einsum("ps,spu->pu", weights, history, preferred_element_type=jnp.float32)


def plain_device(
    statistic_now, statistic_prev, spectral_now, spectral_prev, statistic_hist, spectral_hist
):
    mode_count, time_count = statistic_now.shape
    hist_size = lax.axis_size("hist")
    mom_size = lax.axis_size("mom")
    hist_pos = lax.axis_index("hist")
    mom_pos = lax.axis_index("mom")
    mode_total = mode_count * mom_size
    window = statistic_hist.shape[2]
    sine_rows = sine_table(mode_total)
    frequency = omega_squared(mode_total, mom_pos * mode_count, mode_count)[:, None]
    zero_hist = jnp.zeros((), spectral_hist.dtype)
    times_own = hist_pos * time_count + jnp.arange(time_count)
    times_all = jnp.arange(window)
    lower_mask = times_own[:, None] <= times_all[None, :]
    upper_mask = times_own[:, None] >= times_all[None, :]
    spectral_low = jnp.where(lower_mask[:, None, :], spectral_hist, zero_hist)
    spectral_up = jnp.where(upper_mask[:, None, :], spectral_hist, zero_hist)
    stat_row, stat_old = (statistic_now, statistic_prev)
    spec_row, spec_old = (spectral_now, spectral_prev)
    memory_stat = jnp.zeros_like(statistic_now)
    memory_spec = jnp.zeros_like(spectral_now)
    for step_index in range(STEPS):
        partial_value = lax.psum(jnp.sum(stat_row[:, -1]), "mom")
        edge_total = broadcast(partial_value, "hist", hist_size - 1)
        tadpole = tadpole_coupling * edge_total / mode_total
        padded_stat = stat_row
        padded_spec = spec_row
        gather_stat, gather_spec = (
            lax.all_to_all(padded_stat, "mom", split_axis=1, concat_axis=0, tiled=True),
            lax.all_to_all(padded_spec, "mom", split_axis=1, concat_axis=0, tiled=True),
        )
        pos_stat = jnp.dot(
            sine_rows, gather_stat, precision=highest, preferred_element_type=jnp.float32
        )
        pos_spec = jnp.dot(
            sine_rows, gather_spec, precision=highest, preferred_element_type=jnp.float32
        )
        self_stat_pos, self_spec_pos = self_energy(pos_stat, pos_spec)
        back_stat = jnp.dot(
            sine_rows, self_stat_pos, precision=highest, preferred_element_type=jnp.float32
        ).astype(jnp.bfloat16)
        back_spec = jnp.dot(
            sine_rows, self_spec_pos, precision=highest, preferred_element_type=jnp.float32
        ).astype(jnp.bfloat16)
        modes_stat, modes_spec = (
            lax.all_to_all(back_stat, "mom", split_axis=0, concat_axis=1, tiled=True),
            lax.all_to_all(back_spec, "mom", split_axis=0, concat_axis=1, tiled=True),
        )
        part_stat = contract(modes_spec, statistic_hist) - contract(modes_stat, spectral_low)
        part_spec = contract(modes_spec, spectral_up)
        sum_stat, sum_spec = (
            lax.psum_scatter(part_stat, "hist", scatter_dimension=1, tiled=True),
            lax.psum_scatter(part_spec, "hist", scatter_dimension=1, tiled=True),
        )
        memory_stat = time_step * sum_stat
        memory_spec = time_step * sum_spec
        new_stat = (
            2.0 * stat_row
            - stat_old
            - time_step * time_step * ((frequency + tadpole) * stat_row + memory_stat)
        )
        new_spec = (
            2.0 * spec_row
            - spec_old
            - time_step * time_step * ((frequency + tadpole) * spec_row + memory_spec)
        )
        stat_old, stat_row = (stat_row, new_stat)
        spec_old, spec_row = (spec_row, new_spec)
    return (stat_row, spec_row, memory_stat, memory_spec)


LANES = 128
ROWS = 16
MESH = pl.DeviceIdType.MESH


def copy_to(axis, target, source, landing, send_sem, recv_sem):
    return pltpu.make_async_remote_copy(
        src_ref=source,
        dst_ref=landing,
        send_sem=send_sem,
        recv_sem=recv_sem,
        device_id={axis: target},
        device_id_type=MESH,
    )


def fused_kernel(
    hist_size,
    mom_size,
    stat_now_ref,
    stat_prev_ref,
    spec_now_ref,
    spec_prev_ref,
    stat_hist_ref,
    spec_hist_ref,
    forward_ref,
    back_ref,
    frequency_ref,
    result_ref,
    stat_held,
    spec_held,
    low_mask,
    up_mask,
    spread,
    weights,
    row_send,
    row_recv,
    self_send,
    self_recv,
    part_send,
    part_recv,
    edge_send,
    edge_recv,
    hist_sem,
    row_sem,
    self_sem,
    part_sem,
    edge_sem,
    mode_send,
    mode_recv,
    mode_sem,
    wide_spec,
):
    mode_count, time_count = stat_now_ref.shape
    half = mode_count // 2
    piece = time_count // mom_size
    depth = piece * mode_count
    mode_total = mode_count * mom_size
    here = lax.axis_index("hist")
    me = lax.axis_index("mom")
    order = [*range(1, hist_size), 0]
    rounds = 4 if mom_size % 4 == 0 else mom_size
    round_depth = mom_size * depth // rounds
    round_times = time_count // rounds

    loads = {}
    for turn in order:
        column = pl.multiple_of(lax.rem(here + turn, hist_size) * time_count, time_count)
        for which, (whole, held) in enumerate(
            ((stat_hist_ref, stat_held), (spec_hist_ref, spec_held))
        ):
            loads[turn, which] = pltpu.make_async_copy(
                whole.at[:, pl.ds(column, time_count)], held.at[turn], hist_sem.at[which, turn]
            )
            loads[turn, which].start()

    barrier = pltpu.get_barrier_semaphore()
    for offset in range(1, mom_size):
        pl.semaphore_signal(
            barrier, 1, device_id={"mom": lax.rem(me + offset, mom_size)}, device_id_type=MESH
        )
    for offset in range(1, hist_size):
        pl.semaphore_signal(
            barrier, 1, device_id={"hist": lax.rem(here + offset, hist_size)}, device_id_type=MESH
        )

    place = lax.broadcasted_iota(jnp.int32, (LANES, depth), 0)
    first = lax.broadcasted_iota(jnp.int32, (LANES, depth), 1)
    for kind in range(2):
        for part in range(2):
            start = part * 2 * piece + (1 - kind) * piece
            slot = (place - start) * mode_count
            inside = (first >= slot) & (first < slot + mode_count)
            spread[2 * kind + part] = jnp.where(
                inside, 1.0 if kind == 0 else -1.0, 0.0
            ).astype(jnp.bfloat16)

    stat_row, stat_old = stat_now_ref[...], stat_prev_ref[...]
    spec_row, spec_old = spec_now_ref[...], spec_prev_ref[...]
    frequency = frequency_ref[pl.ds(pl.multiple_of(me * mode_count, mode_count), mode_count), :][
        :, 0:1
    ]
    lane = lax.broadcasted_iota(jnp.int32, (1, LANES), 1)
    first_half = lane < 2 * piece
    is_stat = (lane & (2 * piece - 1)) < piece
    sends = []

    for step in range(STEPS):
        edge = jnp.broadcast_to(
            jnp.sum(stat_row[:, time_count - 1 : time_count], axis=0, keepdims=True), (8, LANES)
        )
        for target in range(mom_size):
            span = slice(target * piece, (target + 1) * piece)
            row_send[step, target] = jnp.concatenate(
                [
                    stat_row[:half, span],
                    spec_row[:half, span],
                    stat_row[half:, span],
                    spec_row[half:, span],
                ],
                axis=1,
            )
        if step == 0:
            pl.semaphore_wait(barrier, mom_size + hist_size - 2)
        row_copies = []
        for offset in range(1, mom_size):
            target = lax.rem(me + offset, mom_size)
            source = lax.rem(me + mom_size - offset, mom_size)
            out = copy_to(
                "mom",
                target,
                row_send.at[step, target],
                row_recv.at[step, me],
                row_sem.at[0, step, offset],
                row_sem.at[1, step, me],
            )
            out.start()
            sends.append(out)
            row_copies.append(
                copy_to(
                    "mom",
                    target,
                    row_send.at[step, source],
                    row_recv.at[step, source],
                    row_sem.at[0, step, offset],
                    row_sem.at[1, step, source],
                )
            )
        row_recv[step, me] = row_send[step, me]
        mode_send[step] = edge
        mode_recv[step, me] = edge
        mode_copies = []
        for offset in range(1, mom_size):
            target = lax.rem(me + offset, mom_size)
            source = lax.rem(me + mom_size - offset, mom_size)
            out = copy_to(
                "mom",
                target,
                mode_send.at[step],
                mode_recv.at[step, me],
                mode_sem.at[0, step, offset],
                mode_sem.at[1, step, me],
            )
            out.start()
            sends.append(out)
            mode_copies.append(
                copy_to(
                    "mom",
                    target,
                    mode_send.at[step],
                    mode_recv.at[step, source],
                    mode_sem.at[0, step, offset],
                    mode_sem.at[1, step, source],
                )
            )

        if step == 0:
            late = lax.broadcasted_iota(jnp.int32, (depth, time_count), 1) * mode_count
            entry = lax.broadcasted_iota(jnp.int32, (depth, time_count), 0)

            def fill(block, carry):
                row = entry + block * depth
                span = pl.ds(pl.multiple_of(block * depth, depth), depth)
                low_mask[span, :] = jnp.where(row < late + mode_count, 1.0, 0.0).astype(
                    jnp.bfloat16
                )
                up_mask[span, :] = jnp.where(row >= late, 1.0, 0.0).astype(jnp.bfloat16)
                return carry

            lax.fori_loop(0, mom_size, fill, 0)

        for copy in row_copies:
            copy.wait_recv()
        rows = row_recv[step].reshape(mom_size * half, LANES)
        both = jnp.dot(
            forward_ref[...], rows, precision=highest, preferred_element_type=jnp.float32
        )
        chosen = jnp.where(first_half, both[:mode_total], both[mode_total:])
        pos = chosen + pltpu.roll(chosen, 2 * piece, 1)
        swapped = pltpu.roll(pos, piece, 1)
        pos_stat = jnp.where(is_stat, pos, swapped)
        pos_spec = jnp.where(is_stat, swapped, pos)
        self_stat, self_spec = self_energy(pos_stat, pos_spec)
        both = jnp.dot(
            back_ref[...],
            jnp.where(is_stat, self_stat, self_spec),
            precision=highest,
            preferred_element_type=jnp.float32,
        )
        self_rows = jnp.where(first_half, both[: mom_size * half], both[mom_size * half :])
        self_send[step] = self_rows.astype(jnp.bfloat16).reshape(mom_size, half, LANES)
        self_copies = []
        for offset in range(1, mom_size):
            target = lax.rem(me + offset, mom_size)
            source = lax.rem(me + mom_size - offset, mom_size)
            out = copy_to(
                "mom",
                target,
                self_send.at[step, target],
                self_recv.at[step, me],
                self_sem.at[0, step, offset],
                self_sem.at[1, step, me],
            )
            out.start()
            sends.append(out)
            self_copies.append(
                copy_to(
                    "mom",
                    target,
                    self_send.at[step, source],
                    self_recv.at[step, source],
                    self_sem.at[0, step, offset],
                    self_sem.at[1, step, source],
                )
            )
        self_recv[step, me] = self_send[step, me]
        for copy in mode_copies:
            copy.wait_recv()
        edge_total = jnp.sum(mode_recv[step], axis=0)
        edge_send[step] = edge_total
        edge_recv[step, here] = edge_total
        edge_copies = []
        for offset in range(1, hist_size):
            target = lax.rem(here + offset, hist_size)
            source = lax.rem(here + hist_size - offset, hist_size)
            out = copy_to(
                "hist",
                target,
                edge_send.at[step],
                edge_recv.at[step, here],
                edge_sem.at[0, step, offset],
                edge_sem.at[1, step, here],
            )
            out.start()
            sends.append(out)
            edge_copies.append(
                copy_to(
                    "hist",
                    target,
                    edge_send.at[step],
                    edge_recv.at[step, source],
                    edge_sem.at[0, step, offset],
                    edge_sem.at[1, step, source],
                )
            )

        for copy in self_copies:
            copy.wait_recv()

        arrived = self_recv[step].reshape(mom_size * half, LANES)
        mode = lax.broadcasted_iota(jnp.int32, (mom_size * half, depth), 1) & (mode_count - 1)
        owner = lax.broadcasted_iota(jnp.int32, (mom_size * half, depth), 0) & (half - 1)
        for kind in range(2):
            for part in range(2):
                wide = jnp.dot(
                    arrived, spread[2 * kind + part], preferred_element_type=jnp.float32
                )
                wide = jnp.where(mode == owner + part * half, wide, 0.0).astype(jnp.bfloat16)
                begin = kind * mode_count + part * half
                for block in range(mom_size):
                    weights[begin : begin + half, block * depth : (block + 1) * depth] = wide[
                        block * half : (block + 1) * half
                    ]

        def widen(block, carry):
            for part in range(2):
                begin = (2 * part + 1) * piece
                values = self_recv[step, block].astype(jnp.float32)
                for late in range(piece):
                    wide_spec[block * piece + late, part * half : (part + 1) * half, :] = (
                        jnp.broadcast_to(
                            values[:, begin + late : begin + late + 1], (half, LANES)
                        )
                    )
            return carry

        lax.fori_loop(0, mom_size, widen, 0)

        def add_stat(turn, block, total):
            for late in range(round_times):
                when = block * round_times + late
                span = pl.ds(pl.multiple_of(when * mode_count, mode_count), mode_count)
                factor = jnp.concatenate([wide_spec[when]] * (time_count // LANES), axis=1)
                total = total + factor * stat_held[turn, span, :].astype(jnp.float32)
            return total

        zeros = jnp.zeros((mode_count, time_count), jnp.float32)
        part_copies = []
        for turn in order:
            if step == 0:
                loads[turn, 0].wait()
                loads[turn, 1].wait()
            if turn:
                target = lax.rem(here + turn, hist_size)
                source = lax.rem(here + hist_size - turn, hist_size)
                wrapped = (here + turn) // hist_size
                select = pl.multiple_of((1 - wrapped) * mode_count, mode_count)

                def add(block, sums, turn=turn, select=select):
                    span = pl.ds(pl.multiple_of(block * round_depth, round_depth), round_depth)
                    return (
                        add_stat(turn, block, sums[0]),
                        sums[1]
                        + jnp.dot(
                            weights[pl.ds(select, mode_count), span],
                            spec_held[turn, span, :],
                            preferred_element_type=jnp.float32,
                        ),
                    )

                stat_sum, spec_sum = lax.fori_loop(0, rounds, add, (zeros, zeros))
                below = wrapped.astype(jnp.float32)
                part_send[step, turn, 0:mode_count, :] = (
                    stat_sum + (1.0 - below) * spec_sum
                ).astype(jnp.bfloat16)
                part_send[step, turn, mode_count:, :] = (below * spec_sum).astype(jnp.bfloat16)
                out = copy_to(
                    "hist",
                    target,
                    part_send.at[step, turn],
                    part_recv.at[step, here],
                    part_sem.at[0, step, turn],
                    part_sem.at[1, step, here],
                )
                out.start()
                sends.append(out)
                part_copies.append(
                    (
                        source,
                        copy_to(
                            "hist",
                            target,
                            part_send.at[step, turn],
                            part_recv.at[step, source],
                            part_sem.at[0, step, turn],
                            part_sem.at[1, step, source],
                        ),
                    )
                )
            else:

                def add_own(block, sums):
                    span = pl.ds(pl.multiple_of(block * round_depth, round_depth), round_depth)
                    rho = spec_held[0, span, :]
                    own = weights[0:mode_count, span]
                    return (
                        add_stat(0, block, sums[0])
                        + jnp.dot(
                            weights[mode_count:, span],
                            rho * low_mask[span, :],
                            preferred_element_type=jnp.float32,
                        ),
                        sums[1]
                        + jnp.dot(
                            own, rho * up_mask[span, :], preferred_element_type=jnp.float32
                        ),
                    )

                stat_sum, spec_sum = lax.fori_loop(0, rounds, add_own, (zeros, zeros))

        for copy in edge_copies:
            copy.wait_recv()
        tadpole = (tadpole_coupling / mode_total) * edge_recv[step, hist_size - 1][0:1, 0:1]
        for source, copy in part_copies:
            copy.wait_recv()
            stat_sum = stat_sum + part_recv[step, source, 0:mode_count, :].astype(jnp.float32)
            spec_sum = spec_sum + part_recv[step, source, mode_count:, :].astype(jnp.float32)
        memory_stat = time_step * stat_sum
        memory_spec = time_step * spec_sum
        square = time_step * time_step
        stiffness = frequency + tadpole
        new_stat = 2.0 * stat_row - stat_old - square * (stiffness * stat_row + memory_stat)
        new_spec = 2.0 * spec_row - spec_old - square * (stiffness * spec_row + memory_spec)
        stat_old, stat_row = stat_row, new_stat
        spec_old, spec_row = spec_row, new_spec

    for place, value in enumerate((stat_row, spec_row, memory_stat, memory_spec)):
        result_ref[place] = value
    for out in sends:
        out.wait_send()


def split_kernel(packed_ref, *results):
    for place, result in enumerate(results):
        result[...] = packed_ref[place]


def sine_blocks(mode_total, mom_size):
    ordinal = np.arange(mode_total, dtype=np.float64) + 1.0
    sine = np.sqrt(2.0 / (mode_total + 1.0)) * np.sin(
        np.pi * ordinal[:, None] * ordinal[None, :] / (mode_total + 1.0)
    )
    split = sine.reshape(mode_total, mom_size, 2, -1)
    lower = split[:, :, 0, :].reshape(mode_total, -1)
    upper = split[:, :, 1, :].reshape(mode_total, -1)
    forward = np.concatenate([lower, upper], axis=0)
    back = np.concatenate([lower.T, upper.T], axis=0)
    frequency = bare_mass + 4.0 * np.sin(np.pi * ordinal / (2.0 * (mode_total + 1.0))) ** 2
    frequency = np.repeat(frequency[:, None], LANES, axis=1)
    return tuple(np.ascontiguousarray(a, np.float32) for a in (forward, back, frequency))


def per_device(
    statistic_now, statistic_prev, spectral_now, spectral_prev, statistic_hist, spectral_hist
):
    mode_count, time_count = statistic_now.shape
    hist_size = lax.axis_size("hist")
    mom_size = lax.axis_size("mom")
    window = statistic_hist.shape[2]
    piece = time_count // mom_size
    half = mode_count // 2
    fits = (
        4 * piece * mom_size == LANES * mom_size
        and half % ROWS == 0
        and mode_count & (mode_count - 1) == 0
        and time_count % LANES == 0
        and hist_size > 1
        and mom_size > 1
    )
    if not fits:
        return plain_device(
            statistic_now, statistic_prev, spectral_now, spectral_prev, statistic_hist, spectral_hist
        )
    mode_total = mode_count * mom_size
    total = time_count * mode_count
    depth = piece * mode_count
    constants = sine_blocks(mode_total, mom_size)
    vmem = pl.BlockSpec(memory_space=pltpu.VMEM)
    far = pl.BlockSpec(memory_space=pl.ANY)
    dma = pltpu.SemaphoreType.DMA
    packed = pl.pallas_call(
        functools.partial(fused_kernel, hist_size, mom_size),
        out_shape=jax.ShapeDtypeStruct((4, mode_count, time_count), jnp.float32),
        in_specs=[vmem] * 4 + [far] * 2 + [vmem] * 3,
        out_specs=vmem,
        scratch_shapes=[
            pltpu.VMEM((hist_size, total, time_count), jnp.bfloat16),
            pltpu.VMEM((hist_size, total, time_count), jnp.bfloat16),
            pltpu.VMEM((total, time_count), jnp.bfloat16),
            pltpu.VMEM((total, time_count), jnp.bfloat16),
            pltpu.VMEM((4, LANES, depth), jnp.bfloat16),
            pltpu.VMEM((2 * mode_count, total), jnp.bfloat16),
            pltpu.VMEM((STEPS, mom_size, half, LANES), jnp.float32),
            pltpu.VMEM((STEPS, mom_size, half, LANES), jnp.float32),
            pltpu.VMEM((STEPS, mom_size, half, LANES), jnp.bfloat16),
            pltpu.VMEM((STEPS, mom_size, half, LANES), jnp.bfloat16),
            pltpu.VMEM((STEPS, hist_size, 2 * mode_count, time_count), jnp.bfloat16),
            pltpu.VMEM((STEPS, hist_size, 2 * mode_count, time_count), jnp.bfloat16),
            pltpu.VMEM((STEPS, 8, LANES), jnp.float32),
            pltpu.VMEM((STEPS, hist_size, 8, LANES), jnp.float32),
            dma((2, hist_size)),
            dma((2, STEPS, mom_size)),
            dma((2, STEPS, mom_size)),
            dma((2, STEPS, hist_size)),
            dma((2, STEPS, hist_size)),
            pltpu.VMEM((STEPS, 8, LANES), jnp.float32),
            pltpu.VMEM((STEPS, mom_size, 8, LANES), jnp.float32),
            dma((2, STEPS, mom_size)),
            pltpu.VMEM((time_count, mode_count, LANES), jnp.float32),
        ],
        compiler_params=pltpu.CompilerParams(
            collective_id=0, has_side_effects=True, vmem_limit_bytes=56 * 1024 * 1024
        ),
        cost_estimate=pl.CostEstimate(
            flops=STEPS * 6 * total * window, bytes_accessed=4 * total * window, transcendentals=0
        ),
    )(
        statistic_now,
        statistic_prev,
        spectral_now,
        spectral_prev,
        statistic_hist.reshape(total, window),
        spectral_hist.reshape(total, window),
        *constants,
    )
    return pl.pallas_call(
        split_kernel,
        out_shape=(jax.ShapeDtypeStruct((mode_count, time_count), jnp.float32),) * 4,
        in_specs=[vmem],
        out_specs=(vmem,) * 4,
    )(packed)


def solution(mesh):
    placed = (
        P("mom", "hist"),
        P("mom", "hist"),
        P("mom", "hist"),
        P("mom", "hist"),
        P("hist", "mom", None),
        P("hist", "mom", None),
    )
    return jax.shard_map(
        per_device,
        mesh=mesh,
        in_specs=placed,
        out_specs=(P("mom", "hist"), P("mom", "hist"), P("mom", "hist"), P("mom", "hist")),
        check_vma=False,
    )
```

```python
import functools

import jax
import jax.numpy as jnp
import numpy as np
from jax import lax
from jax.experimental import pallas as pl
from jax.experimental.pallas import tpu as pltpu
from jax.sharding import PartitionSpec as P

STEPS = 2


time_step = 0.2
bare_mass = 0.04
cubic_coupling = 1.0 / 6.0
tadpole_coupling = 2.0
highest = lax.Precision.HIGHEST


def broadcast(block, axis, source):
    block = jnp.where(lax.axis_index(axis) == source, block, jnp.zeros_like(block))
    return lax.psum(block, axis)


def sine_table(mode_total):
    ordinal = jnp.arange(mode_total, dtype=jnp.float32) + 1.0
    return jnp.sqrt(2.0 / (mode_total + 1.0)) * jnp.sin(
        jnp.pi * ordinal[:, None] * ordinal[None, :] / (mode_total + 1.0)
    )


def omega_squared(mode_total, offset, amount):
    ordinal = (offset + jnp.arange(amount)).astype(jnp.float32) + 1.0
    return bare_mass + 4.0 * jnp.sin(jnp.pi * ordinal / (2.0 * (mode_total + 1.0))) ** 2


def self_energy(pos_stat, pos_spec):
    square_stat = pos_stat * pos_stat
    square_spec = pos_spec * pos_spec
    return (
        -cubic_coupling * pos_stat * (square_stat - 0.75 * square_spec),
        -cubic_coupling * pos_spec * (3.0 * square_stat - 0.25 * square_spec),
    )


def contract(weights, history):
    return jnp.einsum("ps,spu->pu", weights, history, preferred_element_type=jnp.float32)


def plain_device(
    statistic_now, statistic_prev, spectral_now, spectral_prev, statistic_hist, spectral_hist
):
    mode_count, time_count = statistic_now.shape
    hist_size = lax.axis_size("hist")
    mom_size = lax.axis_size("mom")
    hist_pos = lax.axis_index("hist")
    mom_pos = lax.axis_index("mom")
    mode_total = mode_count * mom_size
    window = statistic_hist.shape[2]
    sine_rows = sine_table(mode_total)
    frequency = omega_squared(mode_total, mom_pos * mode_count, mode_count)[:, None]
    zero_hist = jnp.zeros((), spectral_hist.dtype)
    times_own = hist_pos * time_count + jnp.arange(time_count)
    times_all = jnp.arange(window)
    lower_mask = times_own[:, None] <= times_all[None, :]
    upper_mask = times_own[:, None] >= times_all[None, :]
    spectral_low = jnp.where(lower_mask[:, None, :], spectral_hist, zero_hist)
    spectral_up = jnp.where(upper_mask[:, None, :], spectral_hist, zero_hist)
    stat_row, stat_old = (statistic_now, statistic_prev)
    spec_row, spec_old = (spectral_now, spectral_prev)
    memory_stat = jnp.zeros_like(statistic_now)
    memory_spec = jnp.zeros_like(spectral_now)
    for step_index in range(STEPS):
        partial_value = lax.psum(jnp.sum(stat_row[:, -1]), "mom")
        edge_total = broadcast(partial_value, "hist", hist_size - 1)
        tadpole = tadpole_coupling * edge_total / mode_total
        padded_stat = stat_row
        padded_spec = spec_row
        gather_stat, gather_spec = (
            lax.all_to_all(padded_stat, "mom", split_axis=1, concat_axis=0, tiled=True),
            lax.all_to_all(padded_spec, "mom", split_axis=1, concat_axis=0, tiled=True),
        )
        pos_stat = jnp.dot(
            sine_rows, gather_stat, precision=highest, preferred_element_type=jnp.float32
        )
        pos_spec = jnp.dot(
            sine_rows, gather_spec, precision=highest, preferred_element_type=jnp.float32
        )
        self_stat_pos, self_spec_pos = self_energy(pos_stat, pos_spec)
        back_stat = jnp.dot(
            sine_rows, self_stat_pos, precision=highest, preferred_element_type=jnp.float32
        ).astype(jnp.bfloat16)
        back_spec = jnp.dot(
            sine_rows, self_spec_pos, precision=highest, preferred_element_type=jnp.float32
        ).astype(jnp.bfloat16)
        modes_stat, modes_spec = (
            lax.all_to_all(back_stat, "mom", split_axis=0, concat_axis=1, tiled=True),
            lax.all_to_all(back_spec, "mom", split_axis=0, concat_axis=1, tiled=True),
        )
        part_stat = contract(modes_spec, statistic_hist) - contract(modes_stat, spectral_low)
        part_spec = contract(modes_spec, spectral_up)
        sum_stat, sum_spec = (
            lax.psum_scatter(part_stat, "hist", scatter_dimension=1, tiled=True),
            lax.psum_scatter(part_spec, "hist", scatter_dimension=1, tiled=True),
        )
        memory_stat = time_step * sum_stat
        memory_spec = time_step * sum_spec
        new_stat = (
            2.0 * stat_row
            - stat_old
            - time_step * time_step * ((frequency + tadpole) * stat_row + memory_stat)
        )
        new_spec = (
            2.0 * spec_row
            - spec_old
            - time_step * time_step * ((frequency + tadpole) * spec_row + memory_spec)
        )
        stat_old, stat_row = (stat_row, new_stat)
        spec_old, spec_row = (spec_row, new_spec)
    return (stat_row, spec_row, memory_stat, memory_spec)


LANES = 128
ROWS = 16
MESH = pl.DeviceIdType.MESH


def copy_to(axis, target, source, landing, send_sem, recv_sem):
    return pltpu.make_async_remote_copy(
        src_ref=source,
        dst_ref=landing,
        send_sem=send_sem,
        recv_sem=recv_sem,
        device_id={axis: target},
        device_id_type=MESH,
    )


def fused_kernel(
    hist_size,
    mom_size,
    stat_now_ref,
    stat_prev_ref,
    spec_now_ref,
    spec_prev_ref,
    stat_hist_ref,
    spec_hist_ref,
    forward_ref,
    back_ref,
    frequency_ref,
    result_ref,
    stat_held,
    spec_held,
    low_mask,
    up_mask,
    spread,
    weights,
    row_send,
    row_recv,
    self_send,
    self_recv,
    part_send,
    part_recv,
    edge_send,
    edge_recv,
    hist_sem,
    row_sem,
    self_sem,
    part_sem,
    edge_sem,
    mode_send,
    mode_recv,
    mode_sem,
):
    mode_count, time_count = stat_now_ref.shape
    half = mode_count // 2
    piece = time_count // mom_size
    depth = piece * mode_count
    mode_total = mode_count * mom_size
    here = lax.axis_index("hist")
    me = lax.axis_index("mom")
    order = [*range(1, hist_size), 0]
    rounds = 2 if mom_size % 2 == 0 else 1
    round_depth = mom_size * depth // rounds

    loads = {}
    for turn in order:
        column = pl.multiple_of(lax.rem(here + turn, hist_size) * time_count, time_count)
        for which, (whole, held) in enumerate(
            ((stat_hist_ref, stat_held), (spec_hist_ref, spec_held))
        ):
            loads[turn, which] = pltpu.make_async_copy(
                whole.at[:, pl.ds(column, time_count)], held.at[turn], hist_sem.at[which, turn]
            )
            loads[turn, which].start()

    barrier = pltpu.get_barrier_semaphore()
    for offset in range(1, mom_size):
        pl.semaphore_signal(
            barrier, 1, device_id={"mom": lax.rem(me + offset, mom_size)}, device_id_type=MESH
        )
    for offset in range(1, hist_size):
        pl.semaphore_signal(
            barrier, 1, device_id={"hist": lax.rem(here + offset, hist_size)}, device_id_type=MESH
        )

    place = lax.broadcasted_iota(jnp.int32, (LANES, depth), 0)
    first = lax.broadcasted_iota(jnp.int32, (LANES, depth), 1)
    for kind in range(2):
        for part in range(2):
            start = part * 2 * piece + (1 - kind) * piece
            slot = (place - start) * mode_count
            inside = (first >= slot) & (first < slot + mode_count)
            spread[2 * kind + part] = jnp.where(
                inside, 1.0 if kind == 0 else -1.0, 0.0
            ).astype(jnp.bfloat16)

    stat_row, stat_old = stat_now_ref[...], stat_prev_ref[...]
    spec_row, spec_old = spec_now_ref[...], spec_prev_ref[...]
    frequency = frequency_ref[pl.ds(pl.multiple_of(me * mode_count, mode_count), mode_count), :][
        :, 0:1
    ]
    lane = lax.broadcasted_iota(jnp.int32, (1, LANES), 1)
    first_half = lane < 2 * piece
    is_stat = (lane & (2 * piece - 1)) < piece
    sends = []

    for step in range(STEPS):
        edge = jnp.broadcast_to(
            jnp.sum(stat_row[:, time_count - 1 : time_count], axis=0, keepdims=True), (8, LANES)
        )
        for target in range(mom_size):
            span = slice(target * piece, (target + 1) * piece)
            row_send[step, target] = jnp.concatenate(
                [
                    stat_row[:half, span],
                    spec_row[:half, span],
                    stat_row[half:, span],
                    spec_row[half:, span],
                ],
                axis=1,
            )
        if step == 0:
            pl.semaphore_wait(barrier, mom_size + hist_size - 2)
        row_copies = []
        for offset in range(1, mom_size):
            target = lax.rem(me + offset, mom_size)
            source = lax.rem(me + mom_size - offset, mom_size)
            out = copy_to(
                "mom",
                target,
                row_send.at[step, target],
                row_recv.at[step, me],
                row_sem.at[0, step, offset],
                row_sem.at[1, step, me],
            )
            out.start()
            sends.append(out)
            row_copies.append(
                copy_to(
                    "mom",
                    target,
                    row_send.at[step, source],
                    row_recv.at[step, source],
                    row_sem.at[0, step, offset],
                    row_sem.at[1, step, source],
                )
            )
        row_recv[step, me] = row_send[step, me]
        mode_send[step] = edge
        mode_recv[step, me] = edge
        mode_copies = []
        for offset in range(1, mom_size):
            target = lax.rem(me + offset, mom_size)
            source = lax.rem(me + mom_size - offset, mom_size)
            out = copy_to(
                "mom",
                target,
                mode_send.at[step],
                mode_recv.at[step, me],
                mode_sem.at[0, step, offset],
                mode_sem.at[1, step, me],
            )
            out.start()
            sends.append(out)
            mode_copies.append(
                copy_to(
                    "mom",
                    target,
                    mode_send.at[step],
                    mode_recv.at[step, source],
                    mode_sem.at[0, step, offset],
                    mode_sem.at[1, step, source],
                )
            )

        if step == 0:
            late = lax.broadcasted_iota(jnp.int32, (depth, time_count), 1) * mode_count
            entry = lax.broadcasted_iota(jnp.int32, (depth, time_count), 0)

            def fill(block, carry):
                row = entry + block * depth
                span = pl.ds(pl.multiple_of(block * depth, depth), depth)
                low_mask[span, :] = jnp.where(row < late + mode_count, 1.0, 0.0).astype(
                    jnp.bfloat16
                )
                up_mask[span, :] = jnp.where(row >= late, 1.0, 0.0).astype(jnp.bfloat16)
                return carry

            lax.fori_loop(0, mom_size, fill, 0)

        for copy in row_copies:
            copy.wait_recv()
        rows = row_recv[step].reshape(mom_size * half, LANES)
        both = jnp.dot(
            forward_ref[...], rows, precision=highest, preferred_element_type=jnp.float32
        )
        chosen = jnp.where(first_half, both[:mode_total], both[mode_total:])
        pos = chosen + pltpu.roll(chosen, 2 * piece, 1)
        swapped = pltpu.roll(pos, piece, 1)
        pos_stat = jnp.where(is_stat, pos, swapped)
        pos_spec = jnp.where(is_stat, swapped, pos)
        self_stat, self_spec = self_energy(pos_stat, pos_spec)
        both = jnp.dot(
            back_ref[...],
            jnp.where(is_stat, self_stat, self_spec),
            precision=highest,
            preferred_element_type=jnp.float32,
        )
        self_rows = jnp.where(first_half, both[: mom_size * half], both[mom_size * half :])
        self_send[step] = self_rows.astype(jnp.bfloat16).reshape(mom_size, half, LANES)
        self_copies = []
        for offset in range(1, mom_size):
            target = lax.rem(me + offset, mom_size)
            source = lax.rem(me + mom_size - offset, mom_size)
            out = copy_to(
                "mom",
                target,
                self_send.at[step, target],
                self_recv.at[step, me],
                self_sem.at[0, step, offset],
                self_sem.at[1, step, me],
            )
            out.start()
            sends.append(out)
            self_copies.append(
                copy_to(
                    "mom",
                    target,
                    self_send.at[step, source],
                    self_recv.at[step, source],
                    self_sem.at[0, step, offset],
                    self_sem.at[1, step, source],
                )
            )
        self_recv[step, me] = self_send[step, me]
        for copy in mode_copies:
            copy.wait_recv()
        edge_total = jnp.sum(mode_recv[step], axis=0)
        edge_send[step] = edge_total
        edge_recv[step, here] = edge_total
        edge_copies = []
        for offset in range(1, hist_size):
            target = lax.rem(here + offset, hist_size)
            source = lax.rem(here + hist_size - offset, hist_size)
            out = copy_to(
                "hist",
                target,
                edge_send.at[step],
                edge_recv.at[step, here],
                edge_sem.at[0, step, offset],
                edge_sem.at[1, step, here],
            )
            out.start()
            sends.append(out)
            edge_copies.append(
                copy_to(
                    "hist",
                    target,
                    edge_send.at[step],
                    edge_recv.at[step, source],
                    edge_sem.at[0, step, offset],
                    edge_sem.at[1, step, source],
                )
            )

        for copy in self_copies:
            copy.wait_recv()

        arrived = self_recv[step].reshape(mom_size * half, LANES)
        mode = lax.broadcasted_iota(jnp.int32, (mom_size * half, depth), 1) & (mode_count - 1)
        owner = lax.broadcasted_iota(jnp.int32, (mom_size * half, depth), 0) & (half - 1)
        for kind in range(2):
            for part in range(2):
                wide = jnp.dot(
                    arrived, spread[2 * kind + part], preferred_element_type=jnp.float32
                )
                wide = jnp.where(mode == owner + part * half, wide, 0.0).astype(jnp.bfloat16)
                begin = kind * mode_count + part * half
                for block in range(mom_size):
                    weights[begin : begin + half, block * depth : (block + 1) * depth] = wide[
                        block * half : (block + 1) * half
                    ]

        zeros = jnp.zeros((mode_count, time_count), jnp.float32)
        part_copies = []
        for turn in order:
            if step == 0:
                loads[turn, 0].wait()
                loads[turn, 1].wait()
            if turn:
                target = lax.rem(here + turn, hist_size)
                source = lax.rem(here + hist_size - turn, hist_size)
                wrapped = (here + turn) // hist_size
                select = pl.multiple_of((1 - wrapped) * mode_count, mode_count)

                def add(block, sums):
                    span = pl.ds(pl.multiple_of(block * round_depth, round_depth), round_depth)
                    return (
                        sums[0]
                        + jnp.dot(
                            weights[0:mode_count, span],
                            stat_held[turn, span, :],
                            preferred_element_type=jnp.float32,
                        ),
                        sums[1]
                        + jnp.dot(
                            weights[pl.ds(select, mode_count), span],
                            spec_held[turn, span, :],
                            preferred_element_type=jnp.float32,
                        ),
                    )

                stat_sum, spec_sum = lax.fori_loop(0, rounds, add, (zeros, zeros))
                below = wrapped.astype(jnp.float32)
                part_send[step, turn, 0:mode_count, :] = (
                    stat_sum + (1.0 - below) * spec_sum
                ).astype(jnp.bfloat16)
                part_send[step, turn, mode_count:, :] = (below * spec_sum).astype(jnp.bfloat16)
                out = copy_to(
                    "hist",
                    target,
                    part_send.at[step, turn],
                    part_recv.at[step, here],
                    part_sem.at[0, step, turn],
                    part_sem.at[1, step, here],
                )
                out.start()
                sends.append(out)
                part_copies.append(
                    (
                        source,
                        copy_to(
                            "hist",
                            target,
                            part_send.at[step, turn],
                            part_recv.at[step, source],
                            part_sem.at[0, step, turn],
                            part_sem.at[1, step, source],
                        ),
                    )
                )
            else:

                def add_own(block, sums):
                    span = pl.ds(pl.multiple_of(block * round_depth, round_depth), round_depth)
                    rho = spec_held[0, span, :]
                    own = weights[0:mode_count, span]
                    return (
                        sums[0]
                        + jnp.dot(own, stat_held[0, span, :], preferred_element_type=jnp.float32)
                        + jnp.dot(
                            weights[mode_count:, span],
                            rho * low_mask[span, :],
                            preferred_element_type=jnp.float32,
                        ),
                        sums[1]
                        + jnp.dot(
                            own, rho * up_mask[span, :], preferred_element_type=jnp.float32
                        ),
                    )

                stat_sum, spec_sum = lax.fori_loop(0, rounds, add_own, (zeros, zeros))

        for copy in edge_copies:
            copy.wait_recv()
        tadpole = (tadpole_coupling / mode_total) * edge_recv[step, hist_size - 1][0:1, 0:1]
        for source, copy in part_copies:
            copy.wait_recv()
            stat_sum = stat_sum + part_recv[step, source, 0:mode_count, :].astype(jnp.float32)
            spec_sum = spec_sum + part_recv[step, source, mode_count:, :].astype(jnp.float32)
        memory_stat = time_step * stat_sum
        memory_spec = time_step * spec_sum
        square = time_step * time_step
        stiffness = frequency + tadpole
        new_stat = 2.0 * stat_row - stat_old - square * (stiffness * stat_row + memory_stat)
        new_spec = 2.0 * spec_row - spec_old - square * (stiffness * spec_row + memory_spec)
        stat_old, stat_row = stat_row, new_stat
        spec_old, spec_row = spec_row, new_spec

    for place, value in enumerate((stat_row, spec_row, memory_stat, memory_spec)):
        result_ref[place] = value
    for out in sends:
        out.wait_send()


def split_kernel(packed_ref, *results):
    for place, result in enumerate(results):
        result[...] = packed_ref[place]


def sine_blocks(mode_total, mom_size):
    ordinal = np.arange(mode_total, dtype=np.float64) + 1.0
    sine = np.sqrt(2.0 / (mode_total + 1.0)) * np.sin(
        np.pi * ordinal[:, None] * ordinal[None, :] / (mode_total + 1.0)
    )
    split = sine.reshape(mode_total, mom_size, 2, -1)
    lower = split[:, :, 0, :].reshape(mode_total, -1)
    upper = split[:, :, 1, :].reshape(mode_total, -1)
    forward = np.concatenate([lower, upper], axis=0)
    back = np.concatenate([lower.T, upper.T], axis=0)
    frequency = bare_mass + 4.0 * np.sin(np.pi * ordinal / (2.0 * (mode_total + 1.0))) ** 2
    frequency = np.repeat(frequency[:, None], LANES, axis=1)
    return tuple(np.ascontiguousarray(a, np.float32) for a in (forward, back, frequency))


def per_device(
    statistic_now, statistic_prev, spectral_now, spectral_prev, statistic_hist, spectral_hist
):
    mode_count, time_count = statistic_now.shape
    hist_size = lax.axis_size("hist")
    mom_size = lax.axis_size("mom")
    window = statistic_hist.shape[2]
    piece = time_count // mom_size
    half = mode_count // 2
    fits = (
        4 * piece * mom_size == LANES * mom_size
        and half % ROWS == 0
        and mode_count & (mode_count - 1) == 0
        and time_count % LANES == 0
        and hist_size > 1
        and mom_size > 1
    )
    if not fits:
        return plain_device(
            statistic_now, statistic_prev, spectral_now, spectral_prev, statistic_hist, spectral_hist
        )
    mode_total = mode_count * mom_size
    total = time_count * mode_count
    depth = piece * mode_count
    constants = sine_blocks(mode_total, mom_size)
    vmem = pl.BlockSpec(memory_space=pltpu.VMEM)
    far = pl.BlockSpec(memory_space=pl.ANY)
    dma = pltpu.SemaphoreType.DMA
    packed = pl.pallas_call(
        functools.partial(fused_kernel, hist_size, mom_size),
        out_shape=jax.ShapeDtypeStruct((4, mode_count, time_count), jnp.float32),
        in_specs=[vmem] * 4 + [far] * 2 + [vmem] * 3,
        out_specs=vmem,
        scratch_shapes=[
            pltpu.VMEM((hist_size, total, time_count), jnp.bfloat16),
            pltpu.VMEM((hist_size, total, time_count), jnp.bfloat16),
            pltpu.VMEM((total, time_count), jnp.bfloat16),
            pltpu.VMEM((total, time_count), jnp.bfloat16),
            pltpu.VMEM((4, LANES, depth), jnp.bfloat16),
            pltpu.VMEM((2 * mode_count, total), jnp.bfloat16),
            pltpu.VMEM((STEPS, mom_size, half, LANES), jnp.float32),
            pltpu.VMEM((STEPS, mom_size, half, LANES), jnp.float32),
            pltpu.VMEM((STEPS, mom_size, half, LANES), jnp.bfloat16),
            pltpu.VMEM((STEPS, mom_size, half, LANES), jnp.bfloat16),
            pltpu.VMEM((STEPS, hist_size, 2 * mode_count, time_count), jnp.bfloat16),
            pltpu.VMEM((STEPS, hist_size, 2 * mode_count, time_count), jnp.bfloat16),
            pltpu.VMEM((STEPS, 8, LANES), jnp.float32),
            pltpu.VMEM((STEPS, hist_size, 8, LANES), jnp.float32),
            dma((2, hist_size)),
            dma((2, STEPS, mom_size)),
            dma((2, STEPS, mom_size)),
            dma((2, STEPS, hist_size)),
            dma((2, STEPS, hist_size)),
            pltpu.VMEM((STEPS, 8, LANES), jnp.float32),
            pltpu.VMEM((STEPS, mom_size, 8, LANES), jnp.float32),
            dma((2, STEPS, mom_size)),
        ],
        compiler_params=pltpu.CompilerParams(
            collective_id=0, has_side_effects=True, vmem_limit_bytes=56 * 1024 * 1024
        ),
        cost_estimate=pl.CostEstimate(
            flops=STEPS * 6 * total * window, bytes_accessed=4 * total * window, transcendentals=0
        ),
    )(
        statistic_now,
        statistic_prev,
        spectral_now,
        spectral_prev,
        statistic_hist.reshape(total, window),
        spectral_hist.reshape(total, window),
        *constants,
    )
    return pl.pallas_call(
        split_kernel,
        out_shape=(jax.ShapeDtypeStruct((mode_count, time_count), jnp.float32),) * 4,
        in_specs=[vmem],
        out_specs=(vmem,) * 4,
    )(packed)


def solution(mesh):
    placed = (
        P("mom", "hist"),
        P("mom", "hist"),
        P("mom", "hist"),
        P("mom", "hist"),
        P("hist", "mom", None),
        P("hist", "mom", None),
    )
    return jax.shard_map(
        per_device,
        mesh=mesh,
        in_specs=placed,
        out_specs=(P("mom", "hist"), P("mom", "hist"), P("mom", "hist"), P("mom", "hist")),
        check_vma=False,
    )
```

```python
import functools

import jax
import jax.numpy as jnp
import numpy as np
from jax import lax
from jax.experimental import pallas as pl
from jax.experimental.pallas import tpu as pltpu
from jax.sharding import PartitionSpec as P

STEPS = 2


time_step = 0.2
bare_mass = 0.04
cubic_coupling = 1.0 / 6.0
tadpole_coupling = 2.0
highest = lax.Precision.HIGHEST


def broadcast(block, axis, source):
    block = jnp.where(lax.axis_index(axis) == source, block, jnp.zeros_like(block))
    return lax.psum(block, axis)


def sine_table(mode_total):
    ordinal = jnp.arange(mode_total, dtype=jnp.float32) + 1.0
    return jnp.sqrt(2.0 / (mode_total + 1.0)) * jnp.sin(
        jnp.pi * ordinal[:, None] * ordinal[None, :] / (mode_total + 1.0)
    )


def omega_squared(mode_total, offset, amount):
    ordinal = (offset + jnp.arange(amount)).astype(jnp.float32) + 1.0
    return bare_mass + 4.0 * jnp.sin(jnp.pi * ordinal / (2.0 * (mode_total + 1.0))) ** 2


def self_energy(pos_stat, pos_spec):
    square_stat = pos_stat * pos_stat
    square_spec = pos_spec * pos_spec
    return (
        -cubic_coupling * pos_stat * (square_stat - 0.75 * square_spec),
        -cubic_coupling * pos_spec * (3.0 * square_stat - 0.25 * square_spec),
    )


def contract(weights, history):
    return jnp.einsum("ps,spu->pu", weights, history, preferred_element_type=jnp.float32)


def plain_device(
    statistic_now, statistic_prev, spectral_now, spectral_prev, statistic_hist, spectral_hist
):
    mode_count, time_count = statistic_now.shape
    hist_size = lax.axis_size("hist")
    mom_size = lax.axis_size("mom")
    hist_pos = lax.axis_index("hist")
    mom_pos = lax.axis_index("mom")
    mode_total = mode_count * mom_size
    window = statistic_hist.shape[2]
    sine_rows = sine_table(mode_total)
    frequency = omega_squared(mode_total, mom_pos * mode_count, mode_count)[:, None]
    zero_hist = jnp.zeros((), spectral_hist.dtype)
    times_own = hist_pos * time_count + jnp.arange(time_count)
    times_all = jnp.arange(window)
    lower_mask = times_own[:, None] <= times_all[None, :]
    upper_mask = times_own[:, None] >= times_all[None, :]
    spectral_low = jnp.where(lower_mask[:, None, :], spectral_hist, zero_hist)
    spectral_up = jnp.where(upper_mask[:, None, :], spectral_hist, zero_hist)
    stat_row, stat_old = (statistic_now, statistic_prev)
    spec_row, spec_old = (spectral_now, spectral_prev)
    memory_stat = jnp.zeros_like(statistic_now)
    memory_spec = jnp.zeros_like(spectral_now)
    for step_index in range(STEPS):
        partial_value = lax.psum(jnp.sum(stat_row[:, -1]), "mom")
        edge_total = broadcast(partial_value, "hist", hist_size - 1)
        tadpole = tadpole_coupling * edge_total / mode_total
        padded_stat = stat_row
        padded_spec = spec_row
        gather_stat, gather_spec = (
            lax.all_to_all(padded_stat, "mom", split_axis=1, concat_axis=0, tiled=True),
            lax.all_to_all(padded_spec, "mom", split_axis=1, concat_axis=0, tiled=True),
        )
        pos_stat = jnp.dot(
            sine_rows, gather_stat, precision=highest, preferred_element_type=jnp.float32
        )
        pos_spec = jnp.dot(
            sine_rows, gather_spec, precision=highest, preferred_element_type=jnp.float32
        )
        self_stat_pos, self_spec_pos = self_energy(pos_stat, pos_spec)
        back_stat = jnp.dot(
            sine_rows, self_stat_pos, precision=highest, preferred_element_type=jnp.float32
        ).astype(jnp.bfloat16)
        back_spec = jnp.dot(
            sine_rows, self_spec_pos, precision=highest, preferred_element_type=jnp.float32
        ).astype(jnp.bfloat16)
        modes_stat, modes_spec = (
            lax.all_to_all(back_stat, "mom", split_axis=0, concat_axis=1, tiled=True),
            lax.all_to_all(back_spec, "mom", split_axis=0, concat_axis=1, tiled=True),
        )
        part_stat = contract(modes_spec, statistic_hist) - contract(modes_stat, spectral_low)
        part_spec = contract(modes_spec, spectral_up)
        sum_stat, sum_spec = (
            lax.psum_scatter(part_stat, "hist", scatter_dimension=1, tiled=True),
            lax.psum_scatter(part_spec, "hist", scatter_dimension=1, tiled=True),
        )
        memory_stat = time_step * sum_stat
        memory_spec = time_step * sum_spec
        new_stat = (
            2.0 * stat_row
            - stat_old
            - time_step * time_step * ((frequency + tadpole) * stat_row + memory_stat)
        )
        new_spec = (
            2.0 * spec_row
            - spec_old
            - time_step * time_step * ((frequency + tadpole) * spec_row + memory_spec)
        )
        stat_old, stat_row = (stat_row, new_stat)
        spec_old, spec_row = (spec_row, new_spec)
    return (stat_row, spec_row, memory_stat, memory_spec)


LANES = 128
ROWS = 16
MESH = pl.DeviceIdType.MESH


def copy_to(axis, target, source, landing, send_sem, recv_sem):
    return pltpu.make_async_remote_copy(
        src_ref=source,
        dst_ref=landing,
        send_sem=send_sem,
        recv_sem=recv_sem,
        device_id={axis: target},
        device_id_type=MESH,
    )


def fused_kernel(
    hist_size,
    mom_size,
    stat_now_ref,
    stat_prev_ref,
    spec_now_ref,
    spec_prev_ref,
    stat_hist_ref,
    spec_hist_ref,
    forward_far,
    back_far,
    frequency_far,
    result_ref,
    stat_held,
    spec_held,
    low_mask,
    up_mask,
    spread,
    weights,
    row_send,
    row_recv,
    self_send,
    self_recv,
    part_send,
    part_recv,
    edge_send,
    edge_recv,
    hist_sem,
    row_sem,
    self_sem,
    part_sem,
    edge_sem,
    mode_send,
    mode_recv,
    mode_sem,
    forward_ref,
    back_ref,
    frequency_ref,
    table_sem,
):
    mode_count, time_count = stat_now_ref.shape
    half = mode_count // 2
    piece = time_count // mom_size
    depth = piece * mode_count
    mode_total = mode_count * mom_size
    here = lax.axis_index("hist")
    me = lax.axis_index("mom")
    order = [*range(1, hist_size), 0]
    rounds = 1
    round_depth = mom_size * depth // rounds

    tables = [
        pltpu.make_async_copy(whole, held, table_sem.at[place])
        for place, (whole, held) in enumerate(
            (
                (forward_far, forward_ref),
                (back_far, back_ref),
                (frequency_far, frequency_ref),
            )
        )
    ]
    for table in tables:
        table.start()

    loads = {}
    for turn in order:
        column = pl.multiple_of(lax.rem(here + turn, hist_size) * time_count, time_count)
        for which, (whole, held) in enumerate(
            ((stat_hist_ref, stat_held), (spec_hist_ref, spec_held))
        ):
            loads[turn, which] = pltpu.make_async_copy(
                whole.at[:, pl.ds(column, time_count)], held.at[turn], hist_sem.at[which, turn]
            )
            loads[turn, which].start()

    barrier = pltpu.get_barrier_semaphore()
    for offset in range(1, mom_size):
        pl.semaphore_signal(
            barrier, 1, device_id={"mom": lax.rem(me + offset, mom_size)}, device_id_type=MESH
        )
    for offset in range(1, hist_size):
        pl.semaphore_signal(
            barrier, 1, device_id={"hist": lax.rem(here + offset, hist_size)}, device_id_type=MESH
        )

    place = lax.broadcasted_iota(jnp.int32, (LANES, depth), 0)
    first = lax.broadcasted_iota(jnp.int32, (LANES, depth), 1)
    for kind in range(2):
        for part in range(2):
            start = part * 2 * piece + (1 - kind) * piece
            slot = (place - start) * mode_count
            inside = (first >= slot) & (first < slot + mode_count)
            spread[2 * kind + part] = jnp.where(
                inside, 1.0 if kind == 0 else -1.0, 0.0
            ).astype(jnp.bfloat16)

    stat_row, stat_old = stat_now_ref[...], stat_prev_ref[...]
    spec_row, spec_old = spec_now_ref[...], spec_prev_ref[...]
    lane = lax.broadcasted_iota(jnp.int32, (1, LANES), 1)
    first_half = lane < 2 * piece
    is_stat = (lane & (2 * piece - 1)) < piece
    sends = []

    for step in range(STEPS):
        edge = jnp.broadcast_to(
            jnp.sum(stat_row[:, time_count - 1 : time_count], axis=0, keepdims=True), (8, LANES)
        )
        for target in range(mom_size):
            span = slice(target * piece, (target + 1) * piece)
            row_send[step, target] = jnp.concatenate(
                [
                    stat_row[:half, span],
                    spec_row[:half, span],
                    stat_row[half:, span],
                    spec_row[half:, span],
                ],
                axis=1,
            )
        if step == 0:
            pl.semaphore_wait(barrier, mom_size + hist_size - 2)
        row_copies = []
        for offset in range(1, mom_size):
            target = lax.rem(me + offset, mom_size)
            source = lax.rem(me + mom_size - offset, mom_size)
            out = copy_to(
                "mom",
                target,
                row_send.at[step, target],
                row_recv.at[step, me],
                row_sem.at[0, step, offset],
                row_sem.at[1, step, me],
            )
            out.start()
            sends.append(out)
            row_copies.append(
                copy_to(
                    "mom",
                    target,
                    row_send.at[step, source],
                    row_recv.at[step, source],
                    row_sem.at[0, step, offset],
                    row_sem.at[1, step, source],
                )
            )
        row_recv[step, me] = row_send[step, me]
        mode_send[step] = edge
        mode_recv[step, me] = edge
        mode_copies = []
        for offset in range(1, mom_size):
            target = lax.rem(me + offset, mom_size)
            source = lax.rem(me + mom_size - offset, mom_size)
            out = copy_to(
                "mom",
                target,
                mode_send.at[step],
                mode_recv.at[step, me],
                mode_sem.at[0, step, offset],
                mode_sem.at[1, step, me],
            )
            out.start()
            sends.append(out)
            mode_copies.append(
                copy_to(
                    "mom",
                    target,
                    mode_send.at[step],
                    mode_recv.at[step, source],
                    mode_sem.at[0, step, offset],
                    mode_sem.at[1, step, source],
                )
            )

        if step == 0:
            late = lax.broadcasted_iota(jnp.int32, (depth, time_count), 1) * mode_count
            entry = lax.broadcasted_iota(jnp.int32, (depth, time_count), 0)

            def fill(block, carry):
                row = entry + block * depth
                span = pl.ds(pl.multiple_of(block * depth, depth), depth)
                low_mask[span, :] = jnp.where(row < late + mode_count, 1.0, 0.0).astype(
                    jnp.bfloat16
                )
                up_mask[span, :] = jnp.where(row >= late, 1.0, 0.0).astype(jnp.bfloat16)
                return carry

            lax.fori_loop(0, mom_size, fill, 0)

        for copy in row_copies:
            copy.wait_recv()
        if step == 0:
            for table in tables:
                table.wait()
            frequency = frequency_ref[pl.ds(pl.multiple_of(me * mode_count, mode_count), mode_count), :][
                :, 0:1
            ]
        rows = row_recv[step].reshape(mom_size * half, LANES)
        both = jnp.dot(
            forward_ref[...], rows, precision=highest, preferred_element_type=jnp.float32
        )
        chosen = jnp.where(first_half, both[:mode_total], both[mode_total:])
        pos = chosen + pltpu.roll(chosen, 2 * piece, 1)
        swapped = pltpu.roll(pos, piece, 1)
        pos_stat = jnp.where(is_stat, pos, swapped)
        pos_spec = jnp.where(is_stat, swapped, pos)
        self_stat, self_spec = self_energy(pos_stat, pos_spec)
        both = jnp.dot(
            back_ref[...],
            jnp.where(is_stat, self_stat, self_spec),
            precision=highest,
            preferred_element_type=jnp.float32,
        )
        self_rows = jnp.where(first_half, both[: mom_size * half], both[mom_size * half :])
        self_send[step] = self_rows.astype(jnp.bfloat16).reshape(mom_size, half, LANES)
        self_copies = []
        for offset in range(1, mom_size):
            target = lax.rem(me + offset, mom_size)
            source = lax.rem(me + mom_size - offset, mom_size)
            out = copy_to(
                "mom",
                target,
                self_send.at[step, target],
                self_recv.at[step, me],
                self_sem.at[0, step, offset],
                self_sem.at[1, step, me],
            )
            out.start()
            sends.append(out)
            self_copies.append(
                copy_to(
                    "mom",
                    target,
                    self_send.at[step, source],
                    self_recv.at[step, source],
                    self_sem.at[0, step, offset],
                    self_sem.at[1, step, source],
                )
            )
        self_recv[step, me] = self_send[step, me]
        for copy in mode_copies:
            copy.wait_recv()
        edge_total = jnp.sum(mode_recv[step], axis=0)
        edge_send[step] = edge_total
        edge_recv[step, here] = edge_total
        edge_copies = []
        for offset in range(1, hist_size):
            target = lax.rem(here + offset, hist_size)
            source = lax.rem(here + hist_size - offset, hist_size)
            out = copy_to(
                "hist",
                target,
                edge_send.at[step],
                edge_recv.at[step, here],
                edge_sem.at[0, step, offset],
                edge_sem.at[1, step, here],
            )
            out.start()
            sends.append(out)
            edge_copies.append(
                copy_to(
                    "hist",
                    target,
                    edge_send.at[step],
                    edge_recv.at[step, source],
                    edge_sem.at[0, step, offset],
                    edge_sem.at[1, step, source],
                )
            )

        for copy in self_copies:
            copy.wait_recv()

        arrived = self_recv[step].reshape(mom_size * half, LANES)
        mode = lax.broadcasted_iota(jnp.int32, (mom_size * half, depth), 1) & (mode_count - 1)
        owner = lax.broadcasted_iota(jnp.int32, (mom_size * half, depth), 0) & (half - 1)
        for kind in range(2):
            for part in range(2):
                wide = jnp.dot(
                    arrived, spread[2 * kind + part], preferred_element_type=jnp.float32
                )
                wide = jnp.where(mode == owner + part * half, wide, 0.0).astype(jnp.bfloat16)
                begin = kind * mode_count + part * half
                for block in range(mom_size):
                    weights[begin : begin + half, block * depth : (block + 1) * depth] = wide[
                        block * half : (block + 1) * half
                    ]

        zeros = jnp.zeros((mode_count, time_count), jnp.float32)
        part_copies = []
        for turn in order:
            if step == 0:
                loads[turn, 0].wait()
                loads[turn, 1].wait()
            if turn:
                target = lax.rem(here + turn, hist_size)
                source = lax.rem(here + hist_size - turn, hist_size)
                wrapped = (here + turn) // hist_size
                select = pl.multiple_of((1 - wrapped) * mode_count, mode_count)

                def add(block, sums):
                    span = pl.ds(pl.multiple_of(block * round_depth, round_depth), round_depth)
                    return (
                        sums[0]
                        + jnp.dot(
                            weights[0:mode_count, span],
                            stat_held[turn, span, :],
                            preferred_element_type=jnp.float32,
                        ),
                        sums[1]
                        + jnp.dot(
                            weights[pl.ds(select, mode_count), span],
                            spec_held[turn, span, :],
                            preferred_element_type=jnp.float32,
                        ),
                    )

                stat_sum, spec_sum = lax.fori_loop(0, rounds, add, (zeros, zeros))
                below = wrapped.astype(jnp.float32)
                part_send[step, turn, 0:mode_count, :] = (
                    stat_sum + (1.0 - below) * spec_sum
                ).astype(jnp.bfloat16)
                part_send[step, turn, mode_count:, :] = (below * spec_sum).astype(jnp.bfloat16)
                out = copy_to(
                    "hist",
                    target,
                    part_send.at[step, turn],
                    part_recv.at[step, here],
                    part_sem.at[0, step, turn],
                    part_sem.at[1, step, here],
                )
                out.start()
                sends.append(out)
                part_copies.append(
                    (
                        source,
                        copy_to(
                            "hist",
                            target,
                            part_send.at[step, turn],
                            part_recv.at[step, source],
                            part_sem.at[0, step, turn],
                            part_sem.at[1, step, source],
                        ),
                    )
                )
            else:

                def add_own(block, sums):
                    span = pl.ds(pl.multiple_of(block * round_depth, round_depth), round_depth)
                    rho = spec_held[0, span, :]
                    own = weights[0:mode_count, span]
                    return (
                        sums[0]
                        + jnp.dot(own, stat_held[0, span, :], preferred_element_type=jnp.float32)
                        + jnp.dot(
                            weights[mode_count:, span],
                            rho * low_mask[span, :],
                            preferred_element_type=jnp.float32,
                        ),
                        sums[1]
                        + jnp.dot(
                            own, rho * up_mask[span, :], preferred_element_type=jnp.float32
                        ),
                    )

                stat_sum, spec_sum = lax.fori_loop(0, rounds, add_own, (zeros, zeros))

        for copy in edge_copies:
            copy.wait_recv()
        tadpole = (tadpole_coupling / mode_total) * edge_recv[step, hist_size - 1][0:1, 0:1]
        for source, copy in part_copies:
            copy.wait_recv()
            stat_sum = stat_sum + part_recv[step, source, 0:mode_count, :].astype(jnp.float32)
            spec_sum = spec_sum + part_recv[step, source, mode_count:, :].astype(jnp.float32)
        memory_stat = time_step * stat_sum
        memory_spec = time_step * spec_sum
        square = time_step * time_step
        stiffness = frequency + tadpole
        new_stat = 2.0 * stat_row - stat_old - square * (stiffness * stat_row + memory_stat)
        new_spec = 2.0 * spec_row - spec_old - square * (stiffness * spec_row + memory_spec)
        stat_old, stat_row = stat_row, new_stat
        spec_old, spec_row = spec_row, new_spec

    for place, value in enumerate((stat_row, spec_row, memory_stat, memory_spec)):
        result_ref[place] = value
    for out in sends:
        out.wait_send()


def split_kernel(packed_ref, *results):
    for place, result in enumerate(results):
        result[...] = packed_ref[place]


def sine_blocks(mode_total, mom_size):
    ordinal = np.arange(mode_total, dtype=np.float64) + 1.0
    sine = np.sqrt(2.0 / (mode_total + 1.0)) * np.sin(
        np.pi * ordinal[:, None] * ordinal[None, :] / (mode_total + 1.0)
    )
    split = sine.reshape(mode_total, mom_size, 2, -1)
    lower = split[:, :, 0, :].reshape(mode_total, -1)
    upper = split[:, :, 1, :].reshape(mode_total, -1)
    forward = np.concatenate([lower, upper], axis=0)
    back = np.concatenate([lower.T, upper.T], axis=0)
    frequency = bare_mass + 4.0 * np.sin(np.pi * ordinal / (2.0 * (mode_total + 1.0))) ** 2
    frequency = np.repeat(frequency[:, None], LANES, axis=1)
    return tuple(np.ascontiguousarray(a, np.float32) for a in (forward, back, frequency))


def per_device(
    statistic_now, statistic_prev, spectral_now, spectral_prev, statistic_hist, spectral_hist
):
    mode_count, time_count = statistic_now.shape
    hist_size = lax.axis_size("hist")
    mom_size = lax.axis_size("mom")
    window = statistic_hist.shape[2]
    piece = time_count // mom_size
    half = mode_count // 2
    fits = (
        4 * piece * mom_size == LANES * mom_size
        and half % ROWS == 0
        and mode_count & (mode_count - 1) == 0
        and time_count % LANES == 0
        and hist_size > 1
        and mom_size > 1
    )
    if not fits:
        return plain_device(
            statistic_now, statistic_prev, spectral_now, spectral_prev, statistic_hist, spectral_hist
        )
    mode_total = mode_count * mom_size
    total = time_count * mode_count
    depth = piece * mode_count
    constants = sine_blocks(mode_total, mom_size)
    vmem = pl.BlockSpec(memory_space=pltpu.VMEM)
    far = pl.BlockSpec(memory_space=pl.ANY)
    dma = pltpu.SemaphoreType.DMA
    packed = pl.pallas_call(
        functools.partial(fused_kernel, hist_size, mom_size),
        out_shape=jax.ShapeDtypeStruct((4, mode_count, time_count), jnp.float32),
        in_specs=[vmem] * 4 + [far] * 5,
        out_specs=vmem,
        scratch_shapes=[
            pltpu.VMEM((hist_size, total, time_count), jnp.bfloat16),
            pltpu.VMEM((hist_size, total, time_count), jnp.bfloat16),
            pltpu.VMEM((total, time_count), jnp.bfloat16),
            pltpu.VMEM((total, time_count), jnp.bfloat16),
            pltpu.VMEM((4, LANES, depth), jnp.bfloat16),
            pltpu.VMEM((2 * mode_count, total), jnp.bfloat16),
            pltpu.VMEM((STEPS, mom_size, half, LANES), jnp.float32),
            pltpu.VMEM((STEPS, mom_size, half, LANES), jnp.float32),
            pltpu.VMEM((STEPS, mom_size, half, LANES), jnp.bfloat16),
            pltpu.VMEM((STEPS, mom_size, half, LANES), jnp.bfloat16),
            pltpu.VMEM((STEPS, hist_size, 2 * mode_count, time_count), jnp.bfloat16),
            pltpu.VMEM((STEPS, hist_size, 2 * mode_count, time_count), jnp.bfloat16),
            pltpu.VMEM((STEPS, 8, LANES), jnp.float32),
            pltpu.VMEM((STEPS, hist_size, 8, LANES), jnp.float32),
            dma((2, hist_size)),
            dma((2, STEPS, mom_size)),
            dma((2, STEPS, mom_size)),
            dma((2, STEPS, hist_size)),
            dma((2, STEPS, hist_size)),
            pltpu.VMEM((STEPS, 8, LANES), jnp.float32),
            pltpu.VMEM((STEPS, mom_size, 8, LANES), jnp.float32),
            dma((2, STEPS, mom_size)),
            *[pltpu.VMEM(table.shape, jnp.float32) for table in constants],
            dma((3,)),
        ],
        compiler_params=pltpu.CompilerParams(
            collective_id=0, has_side_effects=True, vmem_limit_bytes=56 * 1024 * 1024
        ),
        cost_estimate=pl.CostEstimate(
            flops=STEPS * 6 * total * window, bytes_accessed=4 * total * window, transcendentals=0
        ),
    )(
        statistic_now,
        statistic_prev,
        spectral_now,
        spectral_prev,
        statistic_hist.reshape(total, window),
        spectral_hist.reshape(total, window),
        *constants,
    )
    return pl.pallas_call(
        split_kernel,
        out_shape=(jax.ShapeDtypeStruct((mode_count, time_count), jnp.float32),) * 4,
        in_specs=[vmem],
        out_specs=(vmem,) * 4,
    )(packed)


def solution(mesh):
    placed = (
        P("mom", "hist"),
        P("mom", "hist"),
        P("mom", "hist"),
        P("mom", "hist"),
        P("hist", "mom", None),
        P("hist", "mom", None),
    )
    return jax.shard_map(
        per_device,
        mesh=mesh,
        in_specs=placed,
        out_specs=(P("mom", "hist"), P("mom", "hist"), P("mom", "hist"), P("mom", "hist")),
        check_vma=False,
    )
```
